128 devices in a mesh: group: 4 (over z_hi, core), blk: 32 (over x, y, z_lo).
Axes of the slice: x: 4, y: 4, z: 4 (z_hi: 2, z_lo: 2; z = z_hi * 2 + z_lo), core: 2. Of those that a mesh axis runs over, the one named last changes fastest.
Arguments:
- token_ids: int32 [4, 2, 2048], P('group', None, 'blk'), may hold values from 0 to 31999
- targets: int32 [4, 2, 2048], P('group', None, 'blk'), may hold values from 0 to 31999
- segments: int32 [4, 2, 2048], P('group', None, 'blk'), may hold values from 0 to 7, as said below
- domains: int32 [4, 2, 2048], P('group', None, 'blk'), may hold values from 0 to 4, as said below
- embedding: float32 [4, 32000, 768], P('group', 'blk'), may hold values from -0.4330127 to 0.4330127
- w_rows: float32 [4, 768, 6144], P('group', 'blk'), may hold values from -0.4082483 to 0.4082483
- w_down: float32 [4, 3072, 768], P('group', 'blk'), may hold values from -0.109375 to 0.109375
- norm_gains: float32 [4, 3, 768], P('group', None, 'blk'), may hold values from 0.3 to 2.4
- first_embed: float32 [4, 32000, 768], P('group', 'blk'), may hold values from -1.5258789e-05 to 1.5258789e-05
- first_rows: float32 [4, 768, 6144], P('group', 'blk'), may hold values from -1.5258789e-05 to 1.5258789e-05
- first_down: float32 [4, 3072, 768], P('group', 'blk'), may hold values from -1.5258789e-05 to 1.5258789e-05
- first_gains: float32 [4, 3, 768], P('group', None, 'blk'), may hold values from -6.1035156e-05 to 6.1035156e-05
- second_embed: float32 [4, 32000, 768], P('group', 'blk'), may hold values from 2.0770028e-12 to 3.324784e-11
- second_rows: float32 [4, 768, 6144], P('group', 'blk'), may hold values from 2.0770028e-12 to 3.324784e-11
- second_down: float32 [4, 3072, 768], P('group', 'blk'), may hold values from 2.0770028e-12 to 3.324784e-11
- second_gains: float32 [4, 3, 768], P('group', None, 'blk'), may hold values from 3.324784e-11 to 5.3228133e-10
- delta_embed: float32 [4, 32000, 768], P('group', 'blk'), may hold values from -0.3125 to 0.3125
- delta_rows: float32 [4, 768, 6144], P('group', 'blk'), may hold values from -0.3125 to 0.3125
- delta_down: float32 [4, 3072, 768], P('group', 'blk'), may hold values from -0.3125 to 0.3125
- delta_gains: float32 [4, 3, 768], P('group', None, 'blk'), may hold values from -0.3125 to 0.3125
- outer_embed: float32 [32000, 768], P('blk'), may hold values from -0.3125 to 0.3125
- outer_rows: float32 [768, 6144], P('blk'), may hold values from -0.3125 to 0.3125
- outer_down: float32 [3072, 768], P('blk'), may hold values from -0.3125 to 0.3125
- outer_gains: float32 [3, 768], P(None, 'blk'), may hold values from -0.3125 to 0.3125
Outputs:
- domain_sums: float32 [4, 4], P('group')
- domain_counts: float32 [4, 4], P('group')
- grad_norm: float32 [4], P('group')
- new_embed: float32 [4, 32000, 768], P('group', 'blk')
- new_rows: float32 [4, 768, 6144], P('group', 'blk')
- new_down: float32 [4, 3072, 768], P('group', 'blk')
- new_gains: float32 [4, 3, 768], P('group', None, 'blk')
- moment_embed: float32 [4, 32000, 768], P('group', 'blk')
- moment_rows: float32 [4, 768, 6144], P('group', 'blk')
- moment_down: float32 [4, 3072, 768], P('group', 'blk')
- moment_gains: float32 [4, 3, 768], P('group', None, 'blk')
- square_embed: float32 [4, 32000, 768], P('group', 'blk')
- square_rows: float32 [4, 768, 6144], P('group', 'blk')
- square_down: float32 [4, 3072, 768], P('group', 'blk')
- square_gains: float32 [4, 3, 768], P('group', None, 'blk')
- mean_embed: float32 [32000, 768], P('blk')
- mean_rows: float32 [768, 6144], P('blk')
- mean_down: float32 [3072, 768], P('blk')
- mean_gains: float32 [3, 768], P(None, 'blk')
- momentum_embed: float32 [32000, 768], P('blk')
- momentum_rows: float32 [768, 6144], P('blk')
- momentum_down: float32 [3072, 768], P('blk')
- momentum_gains: float32 [3, 768], P(None, 'blk')
The draws below stay inside these ranges and needn't reach their ends.
Inputs may be any that keep to these rules, and one draw needn't show every extreme that they name: `segments`: segment numbers start at 0 and rise by 0 or 1 from one position to the next within a micro-batch; in one micro-batch of each group a single document fills all 2048 positions, every other micro-batch holds 8 documents. `domains`: every domain below 4 occurs in every micro-batch.
All inputs are finite; a program needn't handle non-finite values.
Results may differ from the reference program's by a relative error of at most 0.012.
The reference program's roundings to bfloat16 on the way count: a program that leaves them out, or rounds other values in their place, can miss the bound.
Values may be sent and summed in bfloat16 or wider, within the bound.
No kernel may reach another device: no remote copies, remote signals or barrier semaphores. Data moves between devices by JAX's collectives and lax.ppermute only.
A program may use at most 320 MiB of HBM per device.

```python
import math
from functools import partial
import jax
import jax.numpy as jnp
import numpy as np
from jax import lax

D = 768
HD = 64
FF = 3072
V = 32000
SEQ = 2048
MICRO = 2
NDOM = 4
STEP = 10
GROUPS = 4


def draw_segments(key, part):
    key = jax.random.fold_in(key, 11)
    key_marks, key_whole = jax.random.split(key)
    index = jnp.arange(SEQ, dtype=jnp.int32)[None, None, :]
    raw_marks = jax.random.randint(key_marks, (GROUPS, MICRO, SEQ), 0, SEQ)
    scores = jnp.where(index > 0, raw_marks * SEQ + index, SEQ * SEQ + index)
    picked = lax.top_k(-scores, 7)[0]
    cutoff = -picked[..., 6:7]
    whole = jax.random.randint(key_whole, (GROUPS, 1, 1), 0, MICRO)
    batch_index = jnp.arange(MICRO, dtype=jnp.int32)[None, :, None]
    cuts = (scores <= cutoff) & (batch_index != whole)
    return jnp.cumsum(cuts.astype(jnp.int32), axis=2).astype(jnp.int32)


def draw_domains(key, part):
    key = jax.random.fold_in(key, 12)
    key_chance, key_kind = jax.random.split(key)
    index = jnp.arange(SEQ, dtype=jnp.int32)[None, None, :]
    chance = jax.random.randint(key_chance, (GROUPS, MICRO, SEQ), 0, 4 * SEQ)
    counted = chance < SEQ + 2 * index
    kind_draw = jax.random.randint(key_kind, (GROUPS, MICRO, SEQ), 0, NDOM)
    span_rows = SEQ // NDOM
    pinned = index % span_rows == 0
    kind_draw = jnp.where(pinned, index // span_rows, kind_draw)
    return jnp.where(counted | pinned, kind_draw, NDOM).astype(jnp.int32)


def draw_embedding(key, part):
    key = jax.random.fold_in(key, 13)
    row_place = jnp.arange(V, dtype=jnp.float32)[None, :, None] / V
    base_draw = jnp.clip(jax.random.normal(key, (GROUPS, V, D), jnp.float32), -4.0, 4.0)
    row_scale = 1.0 + 2.0 * row_place
    return base_draw * row_scale / math.sqrt(D)


def draw_w_rows(key, part):
    key = jax.random.fold_in(key, 14)
    column = jnp.arange(4 * D + FF, dtype=jnp.int32)[None, None, :]
    col_scale = jnp.where((column >= 3 * D) & (column < 4 * D), math.sqrt(8.0), 1.0) / math.sqrt(D)
    base_draw = jnp.clip(jax.random.normal(key, (GROUPS, D, 4 * D + FF), jnp.float32), -4.0, 4.0)
    return base_draw * col_scale


def draw_norm_gains(key, part):
    key = jax.random.fold_in(key, 15)
    column = jnp.arange(D, dtype=jnp.float32)[None, None, :] / D
    ramp = 0.5 + column
    return ramp * jax.random.uniform(key, (GROUPS, 3, D), jnp.float32, 0.85, 1.15)


def touch_ends(drawn, stream_key, least, top_value):
    longest = drawn.shape.index(max(drawn.shape))
    spots = []
    for shift in (0, 1):
        where = [jax.random.randint(jax.random.fold_in(stream_key, axis), (), 0, length) for axis, length in enumerate(drawn.shape)]
        where[longest] = (where[longest] + shift) % drawn.shape[longest]
        spots.append(tuple(where))
    return drawn.at[spots[0]].set(least).at[spots[1]].set(top_value)


def levels(own_key, dims, cuts, low, top_value):
    def one(dim, shards_of):
        draws = jax.random.uniform(jax.random.fold_in(jax.random.fold_in(own_key, 6), dim), (shards_of,), jnp.float32, low / len(cuts), top_value / len(cuts))
        return jnp.repeat(jnp.exp(draws), dims[dim] // shards_of).reshape((-1,) + (1,) * (len(dims) - dim - 1))

    factor_of = one(*cuts[0])
    for cut in cuts[1:]:
        factor_of = factor_of * one(*cut)
    return factor_of


def cumulative_ranks(amount, lean):
    loads = [(1 << 20) // math.isqrt(grade ** lean) + 1 for grade in range(1, amount + 1)]
    width = 1 + sum(loads) // (1 << 30)
    return np.cumsum(np.array([max(1, weight // width) for weight in loads]))


def skewed_ids(rng, shape, count, skew):
    listing = cumulative_ranks(count, skew)
    pick = jax.random.randint(jax.random.fold_in(rng, 1), shape, 0, int(listing[count - 1]))
    rank = jnp.searchsorted(jnp.asarray(listing, jnp.int32), pick, side="right")
    return jax.random.permutation(jax.random.fold_in(rng, 2), count)[rank].astype(jnp.int32)


def centred(stream_key, dims, spread, bound, shards=(), kind=jnp.bfloat16):
    entries = jax.random.normal(stream_key, dims, jnp.float32) * spread
    if len(shards) > 0:
        entries = levels(stream_key, dims, shards, -0.22, 0.18) * entries
    return jnp.clip(entries, min=-bound, max=bound).astype(kind)


def setup_inputs(seed: int = 0) -> dict:
    arg_keys = jax.random.split(jax.random.key(seed), 25)
    return {
        "token_ids": touch_ends(skewed_ids(arg_keys[0], (GROUPS, MICRO, SEQ), V, 2), jax.random.fold_in(arg_keys[0], 3), 0, V - 1).astype(jnp.int32),
        "targets": touch_ends(skewed_ids(arg_keys[1], (GROUPS, MICRO, SEQ), V, 2), jax.random.fold_in(arg_keys[1], 3), 0, V - 1).astype(jnp.int32),
        "segments": draw_segments(jax.random.fold_in(arg_keys[24], 71), 0),
        "domains": draw_domains(jax.random.fold_in(arg_keys[24], 71), 0),
        "embedding": draw_embedding(jax.random.fold_in(arg_keys[24], 71), 0),
        "w_rows": draw_w_rows(jax.random.fold_in(arg_keys[24], 71), 0),
        "w_down": centred(arg_keys[6], (GROUPS, FF, D), FF ** -0.5, 0.109375, ((0, 4), (1, 32)), jnp.float32),
        "norm_gains": draw_norm_gains(jax.random.fold_in(arg_keys[24], 71), 0),
        "first_embed": centred(arg_keys[8], (GROUPS, V, D), (0.111 * 0.05 / (V * D + 4 * D * D + 2 * FF * D + 3 * D) ** 0.5), 1.52587890625e-05, ((0, 4), (1, 32)), jnp.float32),
        "first_rows": centred(arg_keys[9], (GROUPS, D, 4 * D + FF), (0.111 * 0.05 / (V * D + 4 * D * D + 2 * FF * D + 3 * D) ** 0.5), 1.52587890625e-05, ((0, 4), (1, 32)), jnp.float32),
        "first_down": centred(arg_keys[10], (GROUPS, FF, D), (0.111 * 0.05 / (V * D + 4 * D * D + 2 * FF * D + 3 * D) ** 0.5), 1.52587890625e-05, ((0, 4), (1, 32)), jnp.float32),
        "first_gains": centred(arg_keys[11], (GROUPS, 3, D), (0.444 * 0.05 / (V * D + 4 * D * D + 2 * FF * D + 3 * D) ** 0.5), 6.103515625e-05, ((0, 4), (2, 32)), jnp.float32),
        "second_embed": jnp.clip(jnp.exp(math.log(3.324783851010871e-11) - 2.773064 * jax.random.uniform(arg_keys[12], (GROUPS, V, D), jnp.float32) ** levels(arg_keys[12], (GROUPS, V, D), ((0, 4), (1, 32)), -0.2, 0.2)), 2.0770028492239634e-12, 3.324783851010871e-11),
        "second_rows": jnp.clip(jnp.exp(math.log(3.324783851010871e-11) - 2.773064 * jax.random.uniform(arg_keys[13], (GROUPS, D, 4 * D + FF), jnp.float32) ** levels(arg_keys[13], (GROUPS, D, 4 * D + FF), ((0, 4), (1, 32)), -0.2, 0.2)), 2.0770028492239634e-12, 3.324783851010871e-11),
        "second_down": jnp.clip(jnp.exp(math.log(3.324783851010871e-11) - 2.773064 * jax.random.uniform(arg_keys[14], (GROUPS, FF, D), jnp.float32) ** levels(arg_keys[14], (GROUPS, FF, D), ((0, 4), (1, 32)), -0.2, 0.2)), 2.0770028492239634e-12, 3.324783851010871e-11),
        "second_gains": jnp.clip(jnp.exp(math.log(5.322813301233964e-10) - 2.7731824 * jax.random.uniform(arg_keys[15], (GROUPS, 3, D), jnp.float32) ** levels(arg_keys[15], (GROUPS, 3, D), ((0, 4), (2, 32)), -0.2, 0.2)), 3.324783851010871e-11, 5.322813301233964e-10),
        "delta_embed": centred(arg_keys[16], (GROUPS, V, D), 0.02, 0.3125, ((0, 4), (1, 32)), jnp.float32),
        "delta_rows": centred(arg_keys[17], (GROUPS, D, 4 * D + FF), 0.02, 0.3125, ((0, 4), (1, 32)), jnp.float32),
        "delta_down": centred(arg_keys[18], (GROUPS, FF, D), 0.02, 0.3125, ((0, 4), (1, 32)), jnp.float32),
        "delta_gains": centred(arg_keys[19], (GROUPS, 3, D), 0.02, 0.3125, ((0, 4), (2, 32)), jnp.float32),
        "outer_embed": centred(arg_keys[20], (V, D), 0.02, 0.3125, ((0, 32),), jnp.float32),
        "outer_rows": centred(arg_keys[21], (D, 4 * D + FF), 0.02, 0.3125, ((0, 32),), jnp.float32),
        "outer_down": centred(arg_keys[22], (FF, D), 0.02, 0.3125, ((0, 32),), jnp.float32),
        "outer_gains": centred(arg_keys[23], (3, D), 0.02, 0.3125, ((1, 32),), jnp.float32),
    }


EPS = 1e-06
BETA_ONE = 0.9
BETA_TWO = 0.95
ADAM_EPS = 1e-08
DECAY = 0.1
RATE = 0.02
GAIN_RATE = 0.2
CLIP = 0.05
OUTER_RATE = 0.7
OUTER_MU = 0.9
HIGH = lax.Precision.HIGHEST

@jax.custom_vjp
def low(v):
    return lax.optimization_barrier(v.astype(jnp.bfloat16)).astype(jnp.float32)

@jax.custom_vjp
def low_back(v):
    return v

def low_keep(v):
    return (low(v), None)

def low_pass(kept, grad):
    return (grad,)

def back_keep(v):
    return (v, None)

def back_low(kept, grad):
    return (low(grad),)
low.defvjp(low_keep, low_pass)
low_back.defvjp(back_keep, back_low)

def product(left_side, right_side):
    return jnp.dot(left_side, right_side, precision=HIGH, preferred_element_type=jnp.float32)

def rms_norm(values, scales):
    return values * lax.rsqrt(lax.optimization_barrier(jnp.mean(values * values, axis=-1, keepdims=True)) + EPS) * scales

def rotate(values, places):
    half_size = values.shape[-1] // 2
    frequency = jnp.exp(jnp.arange(half_size, dtype=jnp.float32) * (-math.log(10000.0) / half_size))
    angle = places.astype(jnp.float32)[:, None] * frequency[None, :]
    cosine = jnp.cos(angle)[:, None, :]
    sine = jnp.sin(angle)[:, None, :]
    former = values[..., :half_size]
    latter = values[..., half_size:]
    return jnp.concatenate([former * cosine - latter * sine, former * sine + latter * cosine], axis=-1)

def doc_positions(seg_line):
    index = jnp.arange(seg_line.shape[0], dtype=jnp.int32)
    before = jnp.concatenate([jnp.full((1,), -1, jnp.int32), seg_line[:-1]])
    opening = lax.cummax(jnp.where(seg_line != before, index, 0), axis=0)
    return index - opening

def attend(queries, key_rows, value_rows, seg_line):
    seq_length = queries.shape[0]
    head_count = queries.shape[1]
    block_rows = min(512, seq_length)
    all_index = jnp.arange(seq_length, dtype=jnp.int32)

    def one_block(inputs):
        query_block, first_row = inputs
        own_index = first_row + jnp.arange(block_rows, dtype=jnp.int32)
        own_seg = lax.dynamic_slice_in_dim(seg_line, first_row, block_rows)
        raw_scores = jnp.einsum('qhd,khd->hqk', query_block, key_rows, precision=HIGH)
        visible = (all_index[None, :] <= own_index[:, None]) & (seg_line[None, :] == own_seg[:, None])
        scores = jnp.where(visible[None], low_back(raw_scores) * HD ** (-0.5), -1e+30)
        attn_probs = jax.nn.softmax(scores, axis=-1)
        return jnp.einsum('hqk,khd->qhd', low(attn_probs), value_rows, precision=HIGH)
    blocks = queries.reshape(seq_length // block_rows, block_rows, head_count, HD)
    starts = jnp.arange(seq_length // block_rows, dtype=jnp.int32) * block_rows
    return lax.map(jax.checkpoint(one_block), (blocks, starts)).reshape(seq_length, head_count * HD)

def head_losses(normed_out, vocab_table, target_line):
    seq_length = normed_out.shape[0]
    block_rows = min(512, seq_length)

    def one_block(inputs):
        row_block, target_block = inputs
        logits = low_back(jnp.einsum('sd,vd->sv', row_block, vocab_table, precision=HIGH))
        log_total = jax.nn.logsumexp(logits, axis=-1)
        picked = jnp.take_along_axis(logits, target_block[:, None], axis=1)[:, 0]
        return log_total - picked
    losses = lax.map(jax.checkpoint(one_block), (normed_out.reshape(-1, block_rows, D), target_line.reshape(-1, block_rows)))
    return losses.reshape(seq_length)

def forward_group(id_rows, seg_rows, target_rows, weight_rows, params):
    vocab_table = low(params[0])
    rows_weight = low(params[1])
    down_weight = low(params[2])
    gain_weight = low(params[3])
    head_count = D // HD

    def one_sequence(inputs):
        id_line, seg_line, target_line = inputs
        seq_length = id_line.shape[0]
        places = doc_positions(seg_line)
        resid_zero = low_back(jnp.take(vocab_table, id_line, axis=0))
        normed_one = low(rms_norm(resid_zero, gain_weight[0]))
        mixed = low_back(product(normed_one, rows_weight[:, :3 * D]))
        queries = low(rotate(mixed[:, :D].reshape(seq_length, head_count, HD), places))
        key_rows = low(rotate(mixed[:, D:2 * D].reshape(seq_length, head_count, HD), places))
        value_rows = low(mixed[:, 2 * D:].reshape(seq_length, head_count, HD))
        attended = low(low_back(attend(queries, key_rows, value_rows, seg_line)))
        resid_one = resid_zero + low_back(product(attended, rows_weight[:, 3 * D:4 * D]))
        normed_two = low(rms_norm(resid_one, gain_weight[1]))
        upward = low_back(product(normed_two, rows_weight[:, 4 * D:]))
        middle = low(jax.nn.gelu(upward))
        resid_two = resid_one + low_back(product(middle, down_weight))
        normed_out = low(rms_norm(resid_two, gain_weight[2]))
        return head_losses(normed_out, vocab_table, target_line)
    losses = lax.map(one_sequence, (id_rows, seg_rows, target_rows))
    return (jnp.sum(losses * weight_rows), losses)

def adam(weight, gradient, moment, square, step_rate, step_decay):
    moment_new = BETA_ONE * moment + (1.0 - BETA_ONE) * gradient
    square_new = BETA_TWO * square + (1.0 - BETA_TWO) * gradient * gradient
    fixed_moment = moment_new / (1.0 - BETA_ONE ** STEP)
    fixed_square = square_new / (1.0 - BETA_TWO ** STEP)
    moved = weight - step_rate * (fixed_moment / (jnp.sqrt(fixed_square) + ADAM_EPS) + step_decay * weight)
    return (moved, moment_new, square_new)

def reference(token_ids, targets, segments, domains, embedding, w_rows, w_down, norm_gains, first_embed, first_rows, first_down, first_gains, second_embed, second_rows, second_down, second_gains, delta_embed, delta_rows, delta_down, delta_gains, outer_embed, outer_rows, outer_down, outer_gains):
    domain_ids = jnp.arange(NDOM, dtype=jnp.int32)
    means = [lax.optimization_barrier(jnp.sum(delta, axis=0)) / GROUPS for delta in (delta_embed, delta_rows, delta_down, delta_gains)]
    momenta = [OUTER_MU * outer + mean for outer, mean in zip((outer_embed, outer_rows, outer_down, outer_gains), means)]
    sums_list, counts_list, norm_list = ([], [], [])
    new_lists = [[], [], [], []]
    moment_lists = [[], [], [], []]
    square_lists = [[], [], [], []]
    for group_index in range(GROUPS):
        dom_hits = (domains[group_index][..., None] == domain_ids).astype(jnp.float32)
        counts = lax.optimization_barrier(jnp.sum(dom_hits, axis=(0, 1)))
        weight_rows = lax.optimization_barrier(jnp.sum(dom_hits / (NDOM * counts), axis=-1))
        params = (embedding[group_index], w_rows[group_index], w_down[group_index], norm_gains[group_index])
        loss_fn = partial(forward_group, token_ids[group_index], segments[group_index], targets[group_index], weight_rows)
        total_loss, pull_back, losses = jax.vjp(loss_fn, params, has_aux=True)
        gradients = pull_back(jnp.ones_like(total_loss))[0]
        sums_list.append(lax.optimization_barrier(jnp.sum(dom_hits * losses[..., None], axis=(0, 1))))
        counts_list.append(counts)
        squares = sum((jnp.sum(grad_part * grad_part) for grad_part in gradients))
        size_now = jnp.sqrt(squares)
        norm_list.append(size_now)
        factor = jnp.minimum(1.0, CLIP / size_now)
        firsts = (first_embed, first_rows, first_down, first_gains)
        seconds = (second_embed, second_rows, second_down, second_gains)
        for kind_index in range(4):
            step_rate = GAIN_RATE if kind_index == 3 else RATE
            step_decay = 0.0 if kind_index == 3 else DECAY
            moved, moment_new, square_new = adam(params[kind_index], gradients[kind_index] * factor, firsts[kind_index][group_index], seconds[kind_index][group_index], step_rate, step_decay)
            new_lists[kind_index].append(moved - OUTER_RATE * (means[kind_index] + OUTER_MU * momenta[kind_index]))
            moment_lists[kind_index].append(moment_new)
            square_lists[kind_index].append(square_new)
    stacked_new = [jnp.stack(items) for items in new_lists]
    stacked_moment = [jnp.stack(items) for items in moment_lists]
    stacked_square = [jnp.stack(items) for items in square_lists]
    return (jnp.stack(sums_list), jnp.stack(counts_list), jnp.stack(norm_list), stacked_new[0], stacked_new[1], stacked_new[2], stacked_new[3], stacked_moment[0], stacked_moment[1], stacked_moment[2], stacked_moment[3], stacked_square[0], stacked_square[1], stacked_square[2], stacked_square[3], means[0], means[1], means[2], means[3], momenta[0], momenta[1], momenta[2], momenta[3])
```

```python
import functools
import math

import jax
import jax.numpy as jnp
from jax import lax
from jax.experimental import pallas as pl
from jax.experimental.pallas import tpu as pltpu
from jax.sharding import Mesh, PartitionSpec as P

D = 768
HD = 64
NDOM = 4
STEP = 10
SEGS = 8

EPS = 1e-06
BETA_ONE = 0.9
BETA_TWO = 0.95
ADAM_EPS = 1e-08
DECAY = 0.1
RATE = 0.02
GAIN_RATE = 0.2
CLIP = 0.05
OUTER_RATE = 0.7
OUTER_MU = 0.9

NX, NY, NZ = 4, 4, 2
SIZE = {"x": NX, "y": NY, "z": NZ}
PIECE = 128
BLOCK = NX * PIECE
HEADS = D // HD // NX
HW = HEADS * HD
NEG = -1e30

bf16, f32, i32 = jnp.bfloat16, jnp.float32, jnp.int32


def shift(value, axis, step):
    size = SIZE[axis]
    return lax.ppermute(value, axis, [(i, (i + step) % size) for i in range(size)])


def gather_rel(value, axis):
    return [value] + [shift(value, axis, k) for k in range(1, SIZE[axis])]


def scatter_rel(parts, axis):
    return [parts[0]] + [shift(parts[k], axis, -k) for k in range(1, SIZE[axis])]


def sum32(parts):
    total = parts[0].astype(f32)
    for part in parts[1:]:
        total = total + part.astype(f32)
    return total


def all_sum(value):
    for axis in ("z", "y", "x"):
        value = functools.reduce(jnp.add, gather_rel(value, axis))
    return value


def mm(a, b):
    return jnp.dot(a, b, preferred_element_type=f32)


def mm_nt(a, b):
    return lax.dot_general(a, b, (((1,), (1,)), ((), ())), preferred_element_type=f32)


def mm_tn(a, b):
    return lax.dot_general(a, b, (((0,), (0,)), ((), ())), preferred_element_type=f32)


def rms_norm(values, scales):
    return values * lax.rsqrt(jnp.mean(values * values, axis=-1, keepdims=True) + EPS) * scales


def rms_back(values, scales, grad):
    inverse = lax.rsqrt(jnp.mean(values * values, axis=-1, keepdims=True) + EPS)
    unit = values * inverse
    scaled = grad * scales
    grad_values = inverse * (scaled - unit * jnp.mean(scaled * unit, axis=-1, keepdims=True))
    return grad_values, jnp.sum(grad * unit, axis=0)


def swap_halves(values):
    half = HD // 2
    lane = lax.broadcasted_iota(i32, values.shape, 1)
    return jnp.where(
        lane % HD < half, jnp.roll(values, -half, axis=1), jnp.roll(values, half, axis=1)
    )


def visible_keys(idx_q, pos_q, idx_k):
    back = idx_q - idx_k
    return (back >= 0) & (back <= pos_q)


def attend_kernel(q_ref, kv_ref, iq_ref, pq_ref, ik_ref, o_ref, lse_ref):
    mask = visible_keys(iq_ref[...], pq_ref[...], ik_ref[...])
    q, kv = q_ref[...], kv_ref[...]
    outs, tops = [], []
    for h in range(HEADS):
        a, b = h * HD, (h + 1) * HD
        scores = jnp.where(mask, mm_nt(q[:, a:b], kv[:, a:b]) * HD**-0.5, NEG)
        top = jnp.max(scores, axis=1, keepdims=True)
        weight = jnp.exp(scores - top)
        total = jnp.sum(weight, axis=1, keepdims=True)
        probs = (weight * (1.0 / total)).astype(bf16)
        outs.append(mm(probs, kv[:, HW + a : HW + b]))
        tops.append(top + jnp.log(total))
    o_ref[...] = jnp.concatenate(outs, axis=1).astype(bf16)
    lse_ref[...] = jnp.concatenate(tops + [jnp.zeros((tops[0].shape[0], 128 - HEADS), f32)], axis=1)


def attend(q, kv, idx_q, pos_q, idx_k, rows=128):
    n, keys = q.shape[0], kv.shape[0]
    return pl.pallas_call(
        attend_kernel,
        grid=(n // rows,),
        in_specs=[
            pl.BlockSpec((rows, HW), lambda i: (i, 0)),
            pl.BlockSpec((keys, 2 * HW), lambda i: (0, 0)),
            pl.BlockSpec((rows, 1), lambda i: (i, 0)),
            pl.BlockSpec((rows, 1), lambda i: (i, 0)),
            pl.BlockSpec((1, keys), lambda i: (0, 0)),
        ],
        out_specs=[
            pl.BlockSpec((rows, HW), lambda i: (i, 0)),
            pl.BlockSpec((rows, 128), lambda i: (i, 0)),
        ],
        out_shape=[
            jax.ShapeDtypeStruct((n, HW), bf16),
            jax.ShapeDtypeStruct((n, 128), f32),
        ],
        compiler_params=pltpu.CompilerParams(vmem_limit_bytes=40 * 2**20),
        name="attend",
    )(q, kv, idx_q, pos_q, idx_k)


def attend_back_kernel(
    q_ref, kv_ref, iq_ref, pq_ref, ik_ref, lse_ref, do_ref, dq_ref, dkv_ref, acc_ref
):
    step = pl.program_id(0)
    mask = visible_keys(iq_ref[...], pq_ref[...], ik_ref[...])
    q, kv, grad, lse = q_ref[...], kv_ref[...], do_ref[...], lse_ref[...]
    dqs, dks, dvs = [], [], []
    for h in range(HEADS):
        a, b = h * HD, (h + 1) * HD
        key = kv[:, a:b]
        scores = jnp.where(mask, mm_nt(q[:, a:b], key) * HD**-0.5, NEG)
        probs = jnp.exp(scores - lse[:, h : h + 1])
        dprobs = mm_nt(grad[:, a:b], kv[:, HW + a : HW + b])
        row = jnp.sum(probs * dprobs, axis=1, keepdims=True)
        dscores = (probs * (dprobs - row) * HD**-0.5).astype(bf16)
        dqs.append(mm(dscores, key))
        dks.append(mm_tn(dscores, q[:, a:b]))
        dvs.append(mm_tn(probs.astype(bf16), grad[:, a:b]))
    dq_ref[...] = jnp.concatenate(dqs, axis=1)
    part = jnp.concatenate(dks + dvs, axis=1)

    @pl.when(step == 0)
    def _():
        acc_ref[...] = part

    @pl.when(step > 0)
    def _():
        acc_ref[...] += part

    @pl.when(step == pl.num_programs(0) - 1)
    def _():
        dkv_ref[...] = acc_ref[...].astype(bf16)


def attend_back(q, kv, idx_q, pos_q, idx_k, lse, grad, rows=128):
    n, keys = q.shape[0], kv.shape[0]
    return pl.pallas_call(
        attend_back_kernel,
        grid=(n // rows,),
        in_specs=[
            pl.BlockSpec((rows, HW), lambda i: (i, 0)),
            pl.BlockSpec((keys, 2 * HW), lambda i: (0, 0)),
            pl.BlockSpec((rows, 1), lambda i: (i, 0)),
            pl.BlockSpec((rows, 1), lambda i: (i, 0)),
            pl.BlockSpec((1, keys), lambda i: (0, 0)),
            pl.BlockSpec((rows, 128), lambda i: (i, 0)),
            pl.BlockSpec((rows, HW), lambda i: (i, 0)),
        ],
        out_specs=[
            pl.BlockSpec((rows, HW), lambda i: (i, 0)),
            pl.BlockSpec((keys, 2 * HW), lambda i: (0, 0)),
        ],
        out_shape=[
            jax.ShapeDtypeStruct((n, HW), f32),
            jax.ShapeDtypeStruct((keys, 2 * HW), bf16),
        ],
        scratch_shapes=[pltpu.VMEM((keys, 2 * HW), f32)],
        compiler_params=pltpu.CompilerParams(vmem_limit_bytes=48 * 2**20),
        name="attend_back",
    )(q, kv, idx_q, pos_q, idx_k, lse, grad)


def head_kernel(h_ref, e_ref, t_ref, v_ref, p_ref, s_ref):
    logits = mm_nt(h_ref[...], e_ref[...])
    hit = t_ref[...] == v_ref[...]
    top = jnp.max(logits, axis=1, keepdims=True)
    pick = jnp.max(jnp.where(hit, logits, NEG), axis=1, keepdims=True)
    weight = jnp.where(hit, 0.0, jnp.exp(logits - top))
    rest = jnp.sum(weight, axis=1, keepdims=True)
    p_ref[...] = weight.astype(bf16)
    s_ref[...] = jnp.concatenate([top, rest, pick, jnp.zeros((top.shape[0], 125), f32)], axis=1)


def head(hf, table, targets, vocab_ids, rows=256):
    n, v = hf.shape[0], table.shape[0]
    return pl.pallas_call(
        head_kernel,
        grid=(n // rows,),
        in_specs=[
            pl.BlockSpec((rows, D), lambda i: (i, 0)),
            pl.BlockSpec((v, D), lambda i: (0, 0)),
            pl.BlockSpec((rows, 1), lambda i: (i, 0)),
            pl.BlockSpec((1, v), lambda i: (0, 0)),
        ],
        out_specs=[
            pl.BlockSpec((rows, v), lambda i: (i, 0)),
            pl.BlockSpec((rows, 128), lambda i: (i, 0)),
        ],
        out_shape=[
            jax.ShapeDtypeStruct((n, v), bf16),
            jax.ShapeDtypeStruct((n, 128), f32),
        ],
        compiler_params=pltpu.CompilerParams(vmem_limit_bytes=48 * 2**20),
        name="head",
    )(hf, table, targets, vocab_ids)


def adam(weight, gradient, moment, square, step_rate, step_decay):
    moment_new = BETA_ONE * moment + (1.0 - BETA_ONE) * gradient
    square_new = BETA_TWO * square + (1.0 - BETA_TWO) * gradient * gradient
    fixed_moment = moment_new / (1.0 - BETA_ONE**STEP)
    fixed_square = square_new / (1.0 - BETA_TWO**STEP)
    moved = weight - step_rate * (
        fixed_moment / (jnp.sqrt(fixed_square) + ADAM_EPS) + step_decay * weight
    )
    return (moved, moment_new, square_new)


def per_device(
    token_ids,
    targets,
    segments,
    domains,
    embedding,
    w_rows,
    w_down,
    norm_gains,
    first_embed,
    first_rows,
    first_down,
    first_gains,
    second_embed,
    second_rows,
    second_down,
    second_gains,
    delta_embed,
    delta_rows,
    delta_down,
    delta_gains,
    outer_embed,
    outer_rows,
    outer_down,
    outer_gains,
):
    xi, yi, zi = (lax.axis_index(axis) for axis in ("x", "y", "z"))
    mine = (xi * NY + yi) * NZ + zi
    vocab_local = embedding.shape[1]
    ff = w_down.shape[1] * NX * NY * NZ
    ffx = ff // NX

    own_table = embedding[0].astype(bf16)
    table = lax.all_gather(own_table, "x", axis=0, tiled=True)
    owner = (jnp.arange(NX, dtype=i32) * NY + yi) * NZ + zi
    vocab_ids = (owner[:, None] * vocab_local + jnp.arange(vocab_local, dtype=i32)).reshape(-1)

    info = jnp.concatenate([token_ids[0], targets[0], segments[0], domains[0]], axis=0)
    other = shift(info, "z", 1)
    info = jnp.where(
        zi == 0,
        jnp.concatenate([info, other], axis=1),
        jnp.concatenate([other, info], axis=1),
    )
    info = jnp.stack(gather_rel(info, "x"))
    info = jnp.stack(gather_rel(info, "y"))
    info = jnp.transpose(info.reshape(NY, NX, 4, NZ, PIECE), (2, 3, 0, 1, 4))
    info = jnp.where(zi == 0, info, info[:, ::-1])
    counts = jnp.stack([jnp.sum((info[3] == d).astype(f32)) for d in range(NDOM)])

    back_y = jnp.arange(NY, dtype=i32)[:, None, None]
    back_x = jnp.arange(NX, dtype=i32)[None, :, None]
    lane = jnp.arange(PIECE, dtype=i32)[None, None, :]
    place = (((xi - back_x) % NX) * NY + (yi - back_y) % NY) * PIECE + lane
    seg = info[2, 0]
    seg_start = jnp.stack([jnp.sum((seg < s).astype(i32)) for s in range(SEGS)])
    start = sum(jnp.where(seg == s, seg_start[s], 0) for s in range(SEGS))
    idx_k = place.reshape(1, -1)
    idx_q = place[0].reshape(-1, 1)
    pos_q = (place - start)[0].reshape(-1, 1)

    rows_low = w_rows[0].astype(bf16)
    down_low = w_down[0].astype(bf16)
    gains_low = norm_gains[0].astype(bf16)
    rows_in = rows_low.shape[0]

    def by_x(start_col, width):
        block = rows_low[:, start_col : start_col + NX * width]
        return jnp.transpose(block.reshape(rows_in, NX, width), (1, 0, 2))

    cols = jnp.concatenate(
        [by_x(0, HW), by_x(D, HW), by_x(2 * D, HW), by_x(4 * D, ffx)], axis=2
    )
    cols = lax.all_to_all(cols, "x", 0, 0, tiled=True)
    both = jnp.concatenate([rows_low[:, 3 * D : 4 * D], down_low], axis=0)
    gains_pad = jnp.pad(gains_low, ((0, 5), (0, 128 - gains_low.shape[1])))

    def gather_yz(value):
        other = shift(value, "z", 1)
        pair = jnp.where(zi == 0, jnp.stack([value, other]), jnp.stack([other, value]))
        whole = jnp.zeros((NY,) + pair.shape, pair.dtype)
        for k, part in enumerate(gather_rel(pair, "y")):
            whole = lax.dynamic_update_index_in_dim(whole, part, (yi - k) % NY, 0)
        return whole

    cols = gather_yz(cols)
    cols = jnp.transpose(cols, (2, 0, 1, 3, 4)).reshape(D, 3 * HW + ffx)
    w_qkv, w_up = cols[:, : 3 * HW], cols[:, 3 * HW :]
    both = gather_yz(both)
    w_out = both[:, :, :rows_in].reshape(HW, D)
    w_dn = both[:, :, rows_in:].reshape(ffx, D)
    w_outs = gather_rel(w_out, "x")
    gains_yz = gather_yz(gains_pad)
    gains_all = jnp.zeros((NX,) + gains_yz.shape, bf16)
    for k, part in enumerate(gather_rel(gains_yz, "x")):
        gains_all = lax.dynamic_update_index_in_dim(gains_all, part, (xi - k) % NX, 0)
    gain = jnp.transpose(gains_all[..., :3, : gains_low.shape[1]], (3, 0, 1, 2, 4))
    gain = gain.reshape(3, D).astype(f32)

    tokens_t = info[0, :, :, 0].transpose(1, 0, 2).reshape(-1)
    hits = (tokens_t[:, None] == vocab_ids[None, :]).astype(bf16)
    found = mm(hits, table).astype(bf16).reshape(NY, NZ * PIECE, D)
    found = sum32(scatter_rel([found[k] for k in range(NY)], "y")).astype(bf16)
    x0_own = sum32(scatter_rel([found[:PIECE], found[PIECE:]], "z"))
    x0 = jnp.concatenate(gather_rel(x0_own.astype(bf16), "x"), axis=0).astype(f32)

    a = rms_norm(x0, gain[0]).astype(bf16)
    mixed = mm(a, w_qkv)
    frequency = jnp.exp(jnp.arange(HD // 2, dtype=f32) * (-math.log(10000.0) / (HD // 2)))
    angle = pos_q.astype(f32) * frequency[None, :]
    cosine, sine = jnp.cos(angle), jnp.sin(angle)
    cosine = jnp.tile(cosine, (1, 4 * HEADS))
    sine = jnp.tile(jnp.concatenate([-sine, sine], axis=1), (1, 2 * HEADS))
    turned = mixed[:, : 2 * HW]
    turned = (turned * cosine + swap_halves(turned) * sine).astype(bf16)
    q = turned[:, :HW]
    kv = jnp.concatenate([turned[:, HW:], mixed[:, 2 * HW :].astype(bf16)], axis=1)
    kv = jnp.concatenate(gather_rel(kv, "y"), axis=0)
    o, lse_q = attend(q, kv, idx_q, pos_q, idx_k)
    x1 = x0
    for s, heads in enumerate(gather_rel(o, "x")):
        pieces = [heads[((j - s) % NX) * PIECE : ((j - s) % NX + 1) * PIECE] for j in range(NX)]
        heads = jnp.concatenate(pieces, axis=0) if s else heads
        x1 = x1 + mm(heads, w_outs[s])

    b = rms_norm(x1, gain[1]).astype(bf16)
    up = mm(b, w_up)
    hmid = jax.nn.gelu(up).astype(bf16)
    part = mm(hmid, w_dn).astype(bf16).reshape(NX, PIECE, D)
    x2 = x1[:PIECE] + sum32(scatter_rel([part[k] for k in range(NX)], "x"))
    hf = rms_norm(x2, gain[2]).astype(bf16)

    hf_t = jnp.concatenate(gather_rel(hf, "z"), axis=0)
    hf_t = jnp.concatenate(gather_rel(hf_t, "y"), axis=0)
    targets_t = info[1, :, :, 0].transpose(1, 0, 2)
    domains_t = info[3, :, :, 0].transpose(1, 0, 2)
    weight_t = sum(
        jnp.where(domains_t == d, 1.0 / (NDOM * counts[d]), 0.0) for d in range(NDOM)
    ).reshape(NY * NZ, PIECE)
    kept, stats = head(hf_t, table, targets_t.reshape(-1, 1), vocab_ids[None, :])
    stats = stats[:, :3].T.reshape(3, NY, NZ, PIECE)
    all_stats = []
    for kz, by_z in enumerate(gather_rel(stats, "z")):
        by_z = by_z if kz == 0 else by_z[:, :, ::-1]
        all_stats.append(by_z)
    all_stats = jnp.stack(all_stats)
    rolled = [
        jnp.roll(by_y, k, axis=2) if k else by_y
        for k, by_y in enumerate(gather_rel(all_stats, "y"))
    ]
    whole = jnp.concatenate(rolled, axis=0)
    top, rest, pick = whole[:, 0], whole[:, 1], jnp.max(whole[:, 2], axis=0)
    top_all = jnp.max(top, axis=0)
    rest_all = jnp.sum(rest * jnp.exp(top - top_all), axis=0)
    total = rest_all + jnp.exp(pick - top_all)
    log_total = top_all + jnp.log(total)
    ce = log_total - pick
    missing = (rest_all / total).reshape(NY * NZ, PIECE)
    factor_t = jnp.exp(stats[0] - log_total).reshape(NY * NZ, PIECE) * weight_t
    ce_own, dom_own = ce[0, 0], domains_t[0, 0]
    sums_own = jnp.stack([jnp.sum(jnp.where(dom_own == d, ce_own, 0.0)) for d in range(NDOM)])
    hit_t = targets_t.reshape(-1, 1) == vocab_ids[None, :]
    grad_logits = jnp.where(
        hit_t,
        -(weight_t * missing).reshape(-1, 1),
        kept.astype(f32) * factor_t.reshape(-1, 1),
    ).astype(bf16)
    dh = mm(grad_logits, table).astype(bf16).reshape(NY * NZ, PIECE, D)
    terms = [dh[0].astype(f32)]
    for index in range(1, NY * NZ):
        ky, kz = index // NZ, index % NZ
        perm = [
            (y * NZ + z, ((y - ky) % NY) * NZ + (z - kz) % NZ)
            for y in range(NY)
            for z in range(NZ)
        ]
        terms.append(lax.ppermute(dh[index], ("y", "z"), perm))
    d_hf = sum32(terms)
    table_grad = mm_tn(grad_logits, hf_t).astype(bf16)
    table_grad = lax.psum_scatter(table_grad, "x", scatter_dimension=0, tiled=True)

    dx2, gain_two = rms_back(x2, gain[2], d_hf)
    g2 = jnp.concatenate(gather_rel(dx2.astype(bf16), "x"), axis=0)
    unused, pull_gelu = jax.vjp(jax.nn.gelu, up)
    d_up = pull_gelu(mm_nt(g2, w_dn))[0].astype(bf16)
    part = mm_nt(d_up, w_up).astype(bf16).reshape(NX, PIECE, D)
    d_b = sum32(scatter_rel([part[k] for k in range(NX)], "x"))
    down_grad = mm_tn(hmid, g2)
    up_grad = mm_tn(b, d_up)

    def scatter_yz(value):
        return lax.psum_scatter(value, ("y", "z"), scatter_dimension=0, tiled=True)

    def to_yz(value):
        value = value.astype(bf16).reshape(NX, NY * NZ, rows_in, value.shape[1])
        return jnp.transpose(value, (1, 0, 2, 3)).reshape(NY * NZ, NX * rows_in, -1)

    ffn_grad = jnp.concatenate(
        [to_yz(up_grad), down_grad.astype(bf16).reshape(NY * NZ, -1, D)], axis=1
    )
    ffn_grad = scatter_yz(ffn_grad.reshape(-1, D))

    d_norm, gain_one = rms_back(x1[:PIECE], gain[1], d_b)
    dx1 = dx2 + d_norm
    g1 = jnp.concatenate(gather_rel(dx1.astype(bf16), "x"), axis=0)
    d_o = mm_nt(g1, w_out).astype(bf16)
    out_grad = mm_tn(o, g1)
    dq, dkv = attend_back(q, kv, idx_q, pos_q, idx_k, lse_q, d_o)
    dkv = dkv.reshape(NY, BLOCK, 2 * HW)
    dkv = sum32(scatter_rel([dkv[k] for k in range(NY)], "y"))
    d_turned = jnp.concatenate([dq, dkv[:, :HW]], axis=1)
    d_turned = d_turned * cosine - swap_halves(d_turned) * sine
    d_mixed = jnp.concatenate([d_turned, dkv[:, HW:]], axis=1).astype(bf16)
    part = mm_nt(d_mixed, w_qkv).astype(bf16).reshape(NX, PIECE, D)
    d_a = sum32(scatter_rel([part[k] for k in range(NX)], "x"))
    qkv_grad = mm_tn(a, d_mixed)
    qkv_grad = scatter_yz(to_yz(qkv_grad).reshape(-1, 3 * HW))
    out_grad = scatter_yz(out_grad.astype(bf16))
    d_norm, gain_zero = rms_back(x0_own, gain[0], d_a)
    gz = (dx1 + d_norm).astype(bf16)

    gz = jnp.concatenate(gather_rel(gz, "z"), axis=0)
    half = D // 2
    left = jnp.concatenate(gather_rel(gz[:, :half], "x"), axis=0)
    left = jnp.concatenate(gather_rel(left, "y"), axis=0)
    right = gather_rel(jnp.stack(gather_rel(gz[:, half:], "y")), "x")
    right = jnp.stack(right, axis=1).reshape(-1, half)
    gz_all = jnp.concatenate([left, right], axis=1)
    tokens_all = jnp.transpose(info[0], (1, 2, 0, 3)).reshape(-1)
    own_ids = mine * vocab_local + jnp.arange(vocab_local, dtype=i32)
    hits_all = (own_ids[:, None] == tokens_all[None, :]).astype(bf16)
    embed_grad = mm(hits_all, gz_all) + table_grad.astype(f32)

    split = NX * rows_in
    up_part = ffn_grad[:split].reshape(NX, rows_in, ffx)
    down_own = ffn_grad[split:].astype(f32)
    cols_grad = jnp.concatenate([qkv_grad.reshape(NX, rows_in, 3 * HW), up_part], axis=2)
    cols_grad = lax.all_to_all(cols_grad, "x", 0, 0, tiled=True).astype(f32)

    def whole_cols(start_col, width):
        block = cols_grad[:, :, start_col : start_col + width]
        return jnp.transpose(block, (1, 0, 2)).reshape(rows_in, NX * width)

    rows_own = jnp.concatenate(
        [
            whole_cols(0, HW),
            whole_cols(HW, HW),
            whole_cols(2 * HW, HW),
            out_grad.astype(f32),
            whole_cols(3 * HW, ffx),
        ],
        axis=1,
    )

    flat = jnp.concatenate(
        [gain_zero, gain_one, gain_two, sums_own, jnp.zeros((128 - NDOM,), f32)]
    )
    flat = all_sum(flat.reshape(-1, 128)).reshape(-1)
    domain_sums = flat[3 * D : 3 * D + NDOM]
    gains_own = lax.dynamic_slice_in_dim(
        flat[: 3 * D].reshape(3, D), mine * gains_low.shape[1], gains_low.shape[1], 1
    )

    gradients = (embed_grad, rows_own, down_own, gains_own)
    squares = sum(jnp.sum(grad * grad) for grad in gradients)
    squares = all_sum(jnp.broadcast_to(squares, (8, 128)))[0, 0]
    size_now = jnp.sqrt(squares)
    factor = jnp.minimum(1.0, CLIP / size_now)

    summed = lax.psum((delta_embed[0], delta_rows[0], delta_down[0], delta_gains[0]), ("zh", "c"))
    group_count = lax.axis_size("zh") * lax.axis_size("c")
    means = [part_sum / group_count for part_sum in summed]
    momenta = [
        OUTER_MU * outer + mean
        for outer, mean in zip((outer_embed, outer_rows, outer_down, outer_gains), means)
    ]
    weights_now = (embedding[0], w_rows[0], w_down[0], norm_gains[0])
    firsts = (first_embed[0], first_rows[0], first_down[0], first_gains[0])
    seconds = (second_embed[0], second_rows[0], second_down[0], second_gains[0])
    new_items, moment_items, square_items = ([], [], [])
    for kind_index in range(4):
        step_rate = GAIN_RATE if kind_index == 3 else RATE
        step_decay = 0.0 if kind_index == 3 else DECAY
        moved, moment_new, square_new = adam(
            weights_now[kind_index],
            gradients[kind_index] * factor,
            firsts[kind_index],
            seconds[kind_index],
            step_rate,
            step_decay,
        )
        new_items.append(
            (moved - OUTER_RATE * (means[kind_index] + OUTER_MU * momenta[kind_index]))[None]
        )
        moment_items.append(moment_new[None])
        square_items.append(square_new[None])
    return (
        domain_sums[None],
        counts[None],
        size_now.reshape(1),
        *new_items,
        *moment_items,
        *square_items,
        *means,
        *momenta,
    )


def solution(mesh):
    groups = mesh.shape["group"]
    high = 2 if groups % 2 == 0 else 1
    fine = Mesh(
        mesh.devices.reshape(high, groups // high, NX, NY, NZ), ("zh", "c", "x", "y", "z")
    )
    group, blk = ("zh", "c"), ("x", "y", "z")
    tokens = P(group, None, blk)
    rows = P(group, blk, None)
    gains = P(group, None, blk)
    kind = (rows, rows, rows, gains)
    shared = (P(blk, None), P(blk, None), P(blk, None), P(None, blk))
    return jax.shard_map(
        per_device,
        mesh=fine,
        in_specs=(tokens,) * 4 + kind * 4 + shared,
        out_specs=(P(group, None), P(group, None), P(group)) + kind * 3 + shared * 2,
        check_vma=False,
    )
```

```python
import functools
import math

import jax
import jax.numpy as jnp
from jax import lax
from jax.experimental import pallas as pl
from jax.experimental.pallas import tpu as pltpu
from jax.sharding import Mesh, PartitionSpec as P

D = 768
HD = 64
NDOM = 4
STEP = 10
SEGS = 8
PAD = 1024
HALF = D // 2

EPS = 1e-06
BETA_ONE = 0.9
BETA_TWO = 0.95
ADAM_EPS = 1e-08
DECAY = 0.1
RATE = 0.02
GAIN_RATE = 0.2
CLIP = 0.05
OUTER_RATE = 0.7
OUTER_MU = 0.9

NX, NY, NZ = 4, 4, 2
SIZE = {"x": NX, "y": NY, "z": NZ}
PIECE = 128
BLOCK = NX * PIECE
HEADS = D // HD // NX
HW = HEADS * HD
NEG = -1e30

bf16, f32, i32 = jnp.bfloat16, jnp.float32, jnp.int32


def shift(value, axis, step):
    size = SIZE[axis]
    return lax.ppermute(value, axis, [(i, (i + step) % size) for i in range(size)])


def gather_rel(value, axis):
    return [value] + [shift(value, axis, k) for k in range(1, SIZE[axis])]


def scatter_rel(parts, axis):
    return [parts[0]] + [shift(parts[k], axis, -k) for k in range(1, SIZE[axis])]


def gather_ring(value, axis):
    half = value.shape[0] // 2
    before, after = shift(value, axis, 1), shift(value, axis, -1)
    first, second = shift(before[:half], axis, 1), shift(after[half:], axis, -1)
    return [value, before, first, second, after]


def spans(parts):
    start, found = 0, []
    for part in parts:
        found.append((start, start + part.shape[0]))
        start += part.shape[0]
    return found


def sum32(parts):
    total = parts[0].astype(f32)
    for part in parts[1:]:
        total = total + part.astype(f32)
    return total


def all_sum(value):
    for axis in ("z", "y", "x"):
        value = functools.reduce(jnp.add, gather_rel(value, axis))
    return value


def mm(a, b):
    return jnp.dot(a, b, preferred_element_type=f32)


def mm_nt(a, b):
    return lax.dot_general(a, b, (((1,), (1,)), ((), ())), preferred_element_type=f32)


def mm_tn(a, b):
    return lax.dot_general(a, b, (((0,), (0,)), ((), ())), preferred_element_type=f32)


def rms_norm(values, scales):
    return values * lax.rsqrt(jnp.mean(values * values, axis=-1, keepdims=True) + EPS) * scales


def rms_back(values, scales, grad):
    inverse = lax.rsqrt(jnp.mean(values * values, axis=-1, keepdims=True) + EPS)
    unit = values * inverse
    scaled = grad * scales
    grad_values = inverse * (scaled - unit * jnp.mean(scaled * unit, axis=-1, keepdims=True))
    return grad_values, jnp.sum(grad * unit, axis=0)


def tie(values, after):
    return lax.optimization_barrier((values, after))[0]


def turn_lanes(values):
    half = HD // 2
    parts = []
    for start in range(0, values.shape[1], HD):
        parts += [values[:, start + half : start + HD], values[:, start : start + half]]
    return jnp.concatenate(parts, axis=1)


def whole(shape):
    return pl.BlockSpec(shape, lambda *_: (0,) * len(shape))


def fixed(shape):
    return pl.BlockSpec(shape, lambda *_: (0,) * len(shape), pipeline_mode=pl.Buffered(1))


def kernel_params(mib):
    return pltpu.CompilerParams(vmem_limit_bytes=mib * 2**20)


def work(micros):
    return pl.CostEstimate(
        flops=int(micros * 1e9), bytes_accessed=int(micros * 3e6), transcendentals=0
    )


SCALARS = pl.BlockSpec(memory_space=pltpu.SMEM)
ANYWHERE = pl.BlockSpec(memory_space=pl.ANY)


def prep_kernel(
    at_ref, info_ref, base_ref, freq_ref, cols_ref, lists_ref, rows_ref, by_y_ref, by_x_ref, misc_ref, cos_ref, sin_ref
):
    xi, yi, first = at_ref[0], at_ref[1], at_ref[2] == 0

    def tile(y, x):
        halves = []
        for z in range(NZ):
            block = info_ref[(y * NZ + z) * NX + x]
            halves.append(block[:, :64] * 256.0 + block[:, 64:128])
        return jnp.concatenate(halves, axis=1)

    def row(block, kind, other):
        low, high = block[2 * kind : 2 * kind + 1], block[2 * kind + 1 : 2 * kind + 2]
        return jnp.where(first, high, low) if other else jnp.where(first, low, high)

    def lanes(parts):
        return jnp.concatenate(parts, axis=1)

    def pairs(blocks, kind):
        return [row(block, kind, zr) for block in blocks for zr in range(NZ)]

    near = [
        [tile(lax.rem(yi + NY - yb, NY), lax.rem(xi + NX - xb, NX)) for xb in range(NX)]
        for yb in range(NY)
    ]
    flat = [block for line in near for block in line]
    over_y, over_x = [line[0] for line in near], near[0]
    counts = []
    for d in range(NDOM):
        hits = sum(jnp.where(r == float(d), 1.0, 0.0) for r in pairs(flat, 3))
        counts.append(jnp.sum(hits, axis=1, keepdims=True))
    domain = lanes(pairs(over_y, 3))
    weight = jnp.zeros_like(domain)
    for d in range(NDOM):
        weight = jnp.where(domain == float(d), 1.0 / (NDOM * counts[d]), weight)
    lists_ref[...] = lanes(pairs(over_y, 1) + [domain, weight])
    along_y = [tile(y, xi) for y in range(NY)]
    columns = zip(
        pairs(over_y, 0), pairs(over_y, 1), pairs(along_y, 1)
    )
    for k, parts in enumerate(columns):
        square = jnp.concatenate(
            list(parts) + [jnp.zeros((PIECE - len(parts), PIECE), f32)], axis=0
        )
        cols_ref[k * PIECE : (k + 1) * PIECE, :] = jnp.transpose(square).astype(i32)
    seg, seg_own = lanes([row(b, 2, 0) for b in flat]), lanes([row(b, 2, 0) for b in over_x])
    lane = lax.broadcasted_iota(i32, (1, PIECE), 1)
    place = lanes([lane + base_ref[xb] for xb in range(NX)])
    start = jnp.zeros((1, BLOCK), i32)
    for s in range(1, SEGS):
        before = jnp.sum(jnp.where(seg < float(s), 1.0, 0.0), axis=1, keepdims=True)
        start = jnp.where(seg_own == float(s), before.astype(i32), start)
    rows_ref[...] = jnp.concatenate(
        [place, place - start, jnp.zeros((6, BLOCK), i32)], axis=0
    )
    by_x = [near[yb][xb] for xb in range(NX) for yb in range(NY)]
    by_y_ref[...] = lanes(pairs(flat, 0)).astype(i32)
    by_x_ref[...] = lanes(pairs(by_x, 0)).astype(i32)
    misc_ref[...] = jnp.concatenate(
        [jnp.broadcast_to(c, (1, 128)) for c in counts] + [jnp.zeros((4, 128), f32)], axis=0
    )
    angle = (place - start).astype(f32) * freq_ref[:, :1]
    cosine, sine = jnp.cos(angle), jnp.sin(angle)
    cos_ref[...] = jnp.transpose(jnp.concatenate([cosine] * 4, axis=0))
    sin_ref[...] = jnp.transpose(jnp.concatenate([-sine, sine] * 2, axis=0))


def prep(at, info, bases, frequency):
    shapes = [
        ((PAD, 128), i32),
        ((1, 3 * PAD), f32),
        ((8, BLOCK), i32),
        ((1, 4 * PAD), i32),
        ((1, 4 * PAD), i32),
        ((8, 128), f32),
        ((BLOCK, 128), f32),
        ((BLOCK, 128), f32),
    ]
    return pl.pallas_call(
        prep_kernel,
        in_specs=[SCALARS, fixed(info.shape), SCALARS, fixed(frequency.shape)],
        out_specs=[whole(s) for s, _ in shapes],
        out_shape=[jax.ShapeDtypeStruct(s, t) for s, t in shapes],
        grid=(1,),
        compiler_params=kernel_params(12),
        cost_estimate=work(1.4),
        name="prep",
    )(at, info, bases, frequency)


def order_kernel(at_ref, a_ref, b_ref, c_ref, d_ref, out_ref, sem):
    copies = [
        pltpu.make_async_copy(ref, out_ref.at[lax.rem(at_ref[1] + NY - k, NY)], sem.at[k])
        for k, ref in enumerate((a_ref, b_ref, c_ref, d_ref))
    ]
    for copy in copies:
        copy.start()
    for copy in copies:
        copy.wait()


def order_y(at, parts):
    return pl.pallas_call(
        order_kernel,
        in_specs=[SCALARS] + [ANYWHERE] * NY,
        out_specs=ANYWHERE,
        out_shape=jax.ShapeDtypeStruct((NY,) + parts[0].shape, parts[0].dtype),
        scratch_shapes=[pltpu.SemaphoreType.DMA((NY,))],
        compiler_params=kernel_params(4),
        cost_estimate=work(2),
        name="order_y",
    )(at, *parts)


def lookup_kernel(column, base_ref, t_ref, table_ref, out_ref):
    tokens = t_ref[:, column : column + 1]
    total = None
    for k in range(NX):
        ids = lax.broadcasted_iota(i32, (1, PAD), 1) + base_ref[k]
        hit = (tokens == ids).astype(bf16)
        term = mm(hit, table_ref[k * PAD : (k + 1) * PAD, :])
        total = term if total is None else total + term
    out_ref[...] = total.astype(bf16)


def lookup(bases, tokens, column, table, rows=256):
    n = tokens.shape[0]
    return pl.pallas_call(
        functools.partial(lookup_kernel, column),
        grid=(n // rows,),
        in_specs=[
            SCALARS,
            pl.BlockSpec((rows, 128), lambda i: (i, 0)),
            fixed(table.shape),
        ],
        out_specs=pl.BlockSpec((rows, D), lambda i: (i, 0)),
        out_shape=jax.ShapeDtypeStruct((n, D), bf16),
        compiler_params=kernel_params(20),
        cost_estimate=work(10),
        name="lookup",
    )(bases, tokens, table)


def qkv_kernel(
    a_ref, b_ref, c_ref, d_ref, g_ref, w_ref, cos_ref, sin_ref, x_ref, n_ref, q_ref, kv_ref
):
    for k, ref in enumerate((a_ref, b_ref, c_ref, d_ref)):
        rows = slice(k * PIECE, (k + 1) * PIECE)
        x_ref[rows, :] = ref[...]
        normed = rms_norm(ref[...].astype(f32), g_ref[...]).astype(bf16)
        n_ref[rows, :] = normed
        mixed = mm(normed, w_ref[...])
        turned = mixed[:, : 2 * HW]
        cosine = jnp.concatenate([cos_ref[rows, :]] * 3, axis=1)
        sine = jnp.concatenate([sin_ref[rows, :]] * 3, axis=1)
        turned = turned * cosine + turn_lanes(turned) * sine
        q_ref[rows, :] = turned[:, :HW].astype(bf16)
        kv_ref[rows, :] = jnp.concatenate([turned[:, HW:], mixed[:, 2 * HW :]], axis=1).astype(
            bf16
        )


def qkv(pieces, gain, weights, cosine, sine):
    shapes = [(BLOCK, D), (BLOCK, D), (BLOCK, HW), (BLOCK, 2 * HW)]
    return pl.pallas_call(
        qkv_kernel,
        grid=(1,),
        in_specs=[fixed((PIECE, D))] * 4
        + [fixed((1, D)), fixed(weights.shape), fixed(cosine.shape), fixed(sine.shape)],
        out_specs=[whole(s) for s in shapes],
        out_shape=[jax.ShapeDtypeStruct(s, bf16) for s in shapes],
        compiler_params=kernel_params(16),
        cost_estimate=work(2.3),
        name="qkv",
    )(*pieces, gain, weights, cosine, sine)


def qkv_back_kernel(
    dq_ref, a_ref, b_ref, c_ref, d_ref, cos_ref, sin_ref, w_ref, mixed_ref, part_ref
):
    for k in range(NX):
        rows = slice(k * PIECE, (k + 1) * PIECE)
        dkv = sum32([ref[rows, :] for ref in (a_ref, b_ref, c_ref, d_ref)])
        turned = jnp.concatenate([dq_ref[rows, :], dkv[:, :HW]], axis=1)
        cosine = jnp.concatenate([cos_ref[rows, :]] * 3, axis=1)
        sine = jnp.concatenate([sin_ref[rows, :]] * 3, axis=1)
        raw = turned * cosine + turn_lanes(turned * sine)
        mixed = jnp.concatenate([raw, dkv[:, HW:]], axis=1).astype(bf16)
        mixed_ref[rows, :] = mixed
        part_ref[rows, :] = mm_nt(mixed, w_ref[...]).astype(bf16)


def qkv_back(dq, dkvs, cosine, sine, weights):
    shapes = [(BLOCK, 3 * HW), (BLOCK, D)]
    return pl.pallas_call(
        qkv_back_kernel,
        grid=(1,),
        in_specs=[fixed((BLOCK, HW))]
        + [fixed((BLOCK, 2 * HW))] * 4
        + [fixed(cosine.shape), fixed(sine.shape), fixed(weights.shape)],
        out_specs=[whole(s) for s in shapes],
        out_shape=[jax.ShapeDtypeStruct(s, bf16) for s in shapes],
        compiler_params=kernel_params(16),
        cost_estimate=work(2),
        name="qkv_back",
    )(dq, *dkvs, cosine, sine, weights)


def fill_bias(base_ref, rows_ref, bias_ref):
    query, reach = rows_ref[0:1, :], rows_ref[1:2, :]
    key = lax.broadcasted_iota(i32, (PIECE, BLOCK), 0)
    for j in range(NX * NY):
        back = (query - base_ref[j]) - key
        bias_ref[j * PIECE : (j + 1) * PIECE, :] = jnp.where(
            (back >= 0) & (back <= reach), 0.0, NEG
        )


def attend_kernel(
    base_ref, q_ref, a_ref, b_ref, c_ref, d_ref, rows_ref, o_ref, lse_ref, kv_ref, bias_ref
):
    for k, ref in enumerate((a_ref, b_ref, c_ref, d_ref)):
        kv_ref[k * BLOCK : (k + 1) * BLOCK, :] = ref[...]
    fill_bias(base_ref, rows_ref, bias_ref)
    q = q_ref[...] * jnp.asarray(HD**-0.5, bf16)
    outs, tops = [], []
    for h in range(HEADS):
        a, b = h * HD, (h + 1) * HD
        scores = mm_nt(kv_ref[:, a:b], q[:, a:b]) + bias_ref[...]
        top = jnp.max(scores, axis=0, keepdims=True)
        weight = jnp.exp(scores - top)
        total = jnp.sum(weight, axis=0, keepdims=True)
        probs = (weight * (1.0 / total)).astype(bf16)
        outs.append(mm_tn(kv_ref[:, HW + a : HW + b], probs))
        tops.append(top + jnp.log(total))
    o_ref[...] = jnp.transpose(jnp.concatenate(outs, axis=0)).astype(bf16)
    lse_ref[...] = jnp.concatenate(tops + [jnp.zeros((8 - HEADS, BLOCK), f32)], axis=0)


def attend(bases, q, kvs, rows):
    keys = NY * BLOCK
    return pl.pallas_call(
        attend_kernel,
        grid=(1,),
        in_specs=[SCALARS, fixed((BLOCK, HW))]
        + [fixed((BLOCK, 2 * HW))] * 4
        + [fixed((8, BLOCK))],
        out_specs=[whole((BLOCK, HW)), whole((8, BLOCK))],
        out_shape=[
            jax.ShapeDtypeStruct((BLOCK, HW), bf16),
            jax.ShapeDtypeStruct((8, BLOCK), f32),
        ],
        scratch_shapes=[pltpu.VMEM((keys, 2 * HW), bf16), pltpu.VMEM((keys, BLOCK), f32)],
        compiler_params=kernel_params(24),
        cost_estimate=work(8.5),
        name="attend",
    )(bases, q, *kvs, rows)


def attend_back_kernel(
    base_ref,
    q_ref,
    a_ref,
    b_ref,
    c_ref,
    d_ref,
    rows_ref,
    lse_ref,
    ga_ref,
    gb_ref,
    gc_ref,
    gd_ref,
    w_ref,
    dq_ref,
    da_ref,
    db_ref,
    dc_ref,
    dd_ref,
    kv_ref,
    bias_ref,
):
    for k, ref in enumerate((a_ref, b_ref, c_ref, d_ref)):
        kv_ref[k * BLOCK : (k + 1) * BLOCK, :] = ref[...]
    fill_bias(base_ref, rows_ref, bias_ref)
    q = q_ref[...]
    grad = jnp.concatenate(
        [mm_nt(ref[...], w_ref[...]).astype(bf16) for ref in (ga_ref, gb_ref, gc_ref, gd_ref)],
        axis=0,
    )
    scaled = q * jnp.asarray(HD**-0.5, bf16)
    dqs, dks, dvs = [], [], []
    for h in range(HEADS):
        a, b = h * HD, (h + 1) * HD
        key = kv_ref[:, a:b]
        scores = mm_nt(key, scaled[:, a:b]) + bias_ref[...]
        probs = jnp.exp(scores - lse_ref[h : h + 1, :])
        dprobs = mm_nt(kv_ref[:, HW + a : HW + b], grad[:, a:b])
        both = probs * dprobs
        row = jnp.sum(both, axis=0, keepdims=True)
        dscores = ((both - probs * row) * HD**-0.5).astype(bf16)
        dqs.append(mm_tn(key, dscores))
        dks.append(mm(dscores, q[:, a:b]).astype(bf16))
        dvs.append(mm(probs.astype(bf16), grad[:, a:b]).astype(bf16))
    dq_ref[...] = jnp.transpose(jnp.concatenate(dqs, axis=0))
    for k, ref in enumerate((da_ref, db_ref, dc_ref, dd_ref)):
        rows = slice(k * BLOCK, (k + 1) * BLOCK)
        ref[...] = jnp.concatenate([part[rows] for part in dks + dvs], axis=1)


def attend_back(bases, q, kvs, rows, lse, grads, weights):
    keys = NY * BLOCK
    return pl.pallas_call(
        attend_back_kernel,
        grid=(1,),
        in_specs=[SCALARS, fixed((BLOCK, HW))]
        + [fixed((BLOCK, 2 * HW))] * 4
        + [fixed((8, BLOCK)), fixed((8, BLOCK))]
        + [fixed((PIECE, D))] * 4
        + [fixed((HW, D))],
        out_specs=[whole((BLOCK, HW))] + [whole((BLOCK, 2 * HW))] * 4,
        out_shape=[jax.ShapeDtypeStruct((BLOCK, HW), f32)]
        + [jax.ShapeDtypeStruct((BLOCK, 2 * HW), bf16)] * 4,
        scratch_shapes=[pltpu.VMEM((keys, 2 * HW), bf16), pltpu.VMEM((keys, BLOCK), f32)],
        compiler_params=kernel_params(32),
        cost_estimate=work(13.5),
        name="attend_back",
    )(bases, q, *kvs, rows, lse, *grads, weights)


def head_kernel(count, base_ref, *refs):
    states, t_ref, far_ref = refs[:NY], refs[NY], refs[NY + 1]
    outs = refs[NY + 2 : NY + 2 + NY * NZ]
    stats_ref, h_ref, table, sem = refs[NY + 2 + NY * NZ :]
    copy = pltpu.make_async_copy(far_ref, table, sem)
    copy.start()
    rows = states[0].shape[0]
    for k in range(NY):
        h_ref[k * rows : (k + 1) * rows, :] = states[k][...]
    copy.wait()
    targets = t_ref[:, 1:2]
    states = h_ref[...]
    column = lax.broadcasted_iota(i32, (1, PAD), 1)
    top = None
    for k in range(NX):
        block = table[k * PAD : (k + 1) * PAD, :]
        logits = mm_nt(states, block)
        cut = count // 128 * 128
        spare = jnp.where(column[:, cut:] < count, 0.0, NEG)
        logits = jnp.concatenate([logits[:, :cut], logits[:, cut:] + spare], axis=1)
        hit = targets == jnp.where(column < count, column + base_ref[k], -1)
        here = jnp.max(logits, axis=1, keepdims=True)
        found = jnp.max(jnp.where(hit, logits, NEG), axis=1, keepdims=True)
        if top is None:
            top, pick = here, found
            weight = jnp.where(hit, 0.0, jnp.exp(logits - top))
            rest = jnp.sum(weight, axis=1, keepdims=True)
            total = mm(weight.astype(bf16), block)
        else:
            higher = jnp.maximum(top, here)
            scale = jnp.exp(top - higher)
            pick = jnp.maximum(pick, found)
            weight = jnp.where(hit, 0.0, jnp.exp(logits - higher))
            rest = rest * scale + jnp.sum(weight, axis=1, keepdims=True)
            total = total * scale + mm(weight.astype(bf16), block)
            top = higher
    for k, out_ref in enumerate(outs):
        out_ref[...] = total[k * PIECE : (k + 1) * PIECE].astype(bf16)
    stats = jnp.concatenate([top, rest, pick, jnp.zeros((top.shape[0], 125), f32)], axis=1)
    stats = jnp.transpose(stats)[:8, :]
    for k in range(NY * NZ):
        stats_ref[k] = stats


def head(count, bases, states, table, targets):
    n = NY * NZ * PIECE
    return pl.pallas_call(
        functools.partial(head_kernel, count),
        grid=(1,),
        in_specs=[SCALARS]
        + [fixed((n // NY, D))] * NY
        + [fixed((n, 128)), ANYWHERE],
        out_specs=[whole((PIECE, D))] * (NY * NZ) + [whole((NY * NZ, 8, n))],
        out_shape=[jax.ShapeDtypeStruct((PIECE, D), bf16)] * (NY * NZ)
        + [jax.ShapeDtypeStruct((NY * NZ, 8, n), f32)],
        scratch_shapes=[
            pltpu.VMEM((n, D), bf16),
            pltpu.VMEM((NX * PAD, D), bf16),
            pltpu.SemaphoreType.DMA,
        ],
        compiler_params=kernel_params(38),
        cost_estimate=work(20),
        name="head",
    )(bases, *states, targets, table)


def merge_kernel(at_ref, stats_ref, lists_ref, rows_ref, cols_ref, sums_ref):
    n = NY * NZ * PIECE

    def ordered(values, k, kz):
        parts = []
        for l in range(NY):
            for zr in range(NZ):
                at = (((l - k) % NY) * NZ + (zr - kz) % NZ) * PIECE
                parts.append(values[:, at : at + PIECE])
        return jnp.concatenate(parts, axis=1)

    shards = {}
    for k in range(NY):
        for kz in range(NZ):
            y, z = lax.rem(at_ref[1] + NY - k, NY), lax.rem(at_ref[2] + NZ - kz, NZ)
            shards[k, kz] = stats_ref[y * NZ + z]
    shards = {key: ordered(values, *key) for key, values in shards.items()}
    domain, weight = lists_ref[:, n : 2 * n], lists_ref[:, 2 * n : 3 * n]
    top = functools.reduce(jnp.maximum, [s[0:1] for s in shards.values()])
    rest = sum(s[1:2] * jnp.exp(s[0:1] - top) for s in shards.values())
    pick = functools.reduce(jnp.maximum, [s[2:3] for s in shards.values()])
    total = rest + jnp.exp(pick - top)
    lse = top + jnp.log(total)
    missing = weight * (rest / total)
    rows_ref[...] = jnp.concatenate([lse, weight, -missing, jnp.zeros((5, n), f32)], axis=0)
    mine = slice(0, PIECE)
    scales = []
    for ky in range(NY):
        for kz in range(NZ):
            stats = shards[(-ky) % NY, kz]
            scales.append(weight[:, mine] * jnp.exp(stats[0:1, mine] - lse[:, mine]))
    scales += [missing[:, mine], jnp.zeros((128 - len(scales) - 1, PIECE), f32)]
    cols_ref[...] = jnp.transpose(jnp.concatenate(scales, axis=0))
    loss = lse[:, mine] - pick[:, mine]
    lane = lax.broadcasted_iota(i32, (1, 128), 1)
    sums = jnp.zeros((1, 128), f32)
    for d in range(NDOM):
        part = jnp.sum(jnp.where(domain[:, mine] == float(d), loss, 0.0), axis=1, keepdims=True)
        sums = jnp.where(lane == d, part, sums)
    sums_ref[...] = sums


def merge(at, stats, lists):
    n = NY * NZ * PIECE
    return pl.pallas_call(
        merge_kernel,
        grid=(1,),
        in_specs=[SCALARS, fixed(stats.shape), fixed(lists.shape)],
        out_specs=[whole((8, n)), whole((PIECE, 128)), whole((1, 128))],
        out_shape=[
            jax.ShapeDtypeStruct((8, n), f32),
            jax.ShapeDtypeStruct((PIECE, 128), f32),
            jax.ShapeDtypeStruct((1, 128), f32),
        ],
        compiler_params=kernel_params(12),
        cost_estimate=work(1.2),
        name="merge",
    )(at, stats, lists)


def table_grad_kernel(
    chunk, base_ref, e_ref, a_ref, b_ref, c_ref, d_ref, t_ref, s_ref, *refs
):
    out_ref = refs[-1]
    rows = out_ref.shape[0]
    ids = lax.broadcasted_iota(i32, (rows, 1), 0) + (base_ref[chunk] + pl.program_id(0) * rows)
    total = None
    for k, ref in enumerate((a_ref, b_ref, c_ref, d_ref)):
        n = ref.shape[0]
        part = slice(k * n, (k + 1) * n)
        logits = mm_nt(e_ref[...], ref[...])
        grad = jnp.exp(logits - s_ref[0:1, part]) * s_ref[1:2, part]
        grad = jnp.where(ids == t_ref[:, part], s_ref[2:3, part], grad).astype(bf16)
        term = mm(grad, ref[...])
        total = term if total is None else total + term
    out_ref[...] = total.astype(bf16)


def table_grad(chunk, bases, table, states, targets, stats, before=None, rows=512):
    n = NY * NZ * PIECE
    per = PAD // rows
    more = () if before is None else (before,)
    return pl.pallas_call(
        functools.partial(table_grad_kernel, chunk),
        grid=(per,),
        in_specs=[SCALARS]
        + [pl.BlockSpec((rows, D), lambda i: (chunk * per + i, 0))]
        + [fixed((n // NY, D))] * NY
        + [fixed((1, n)), fixed((8, n))]
        + [ANYWHERE] * len(more),
        out_specs=pl.BlockSpec((rows, D), lambda i: (chunk * per + i, 0)),
        out_shape=jax.ShapeDtypeStruct((NX * PAD, D), bf16),
        input_output_aliases={8: 0} if more else {},
        compiler_params=kernel_params(24),
        cost_estimate=work(6.2),
        name="table_grad",
    )(bases, table, *states, targets, stats, *more)


def embed_start_kernel(count, base_ref, t_ref, *refs):
    parts, out_ref = refs[:-1], refs[-1]
    rows = out_ref.shape[0]
    row = lax.broadcasted_iota(i32, (rows, 1), 0) + pl.program_id(0) * rows
    ids = jnp.where(row < count, row + base_ref[0], -1)
    total = None
    for ref, low in zip(parts, (0, PAD, 3 * PAD)):
        hit = (ids == t_ref[:, low : low + PAD]).astype(bf16)
        term = mm(hit, ref[...])
        total = term if total is None else total + term
    out_ref[...] = total


def embed_start(count, base, tokens, parts, rows=256):
    width = parts[0].shape[1]
    return pl.pallas_call(
        functools.partial(embed_start_kernel, count),
        grid=(PAD // rows,),
        in_specs=[SCALARS, fixed(tokens.shape)] + [fixed(part.shape) for part in parts],
        out_specs=pl.BlockSpec((rows, width), lambda i: (i, 0)),
        out_shape=jax.ShapeDtypeStruct((PAD, width), f32),
        compiler_params=kernel_params(24),
        cost_estimate=work(4),
        name="embed_start",
    )(base, tokens, *parts)


def embed_end_kernel(
    count, base_ref, ty_ref, tx_ref, a_ref, b_ref, c_ref, d_ref, l_ref, r_ref, h_ref, m_ref, out_ref, sum_ref
):
    rows = out_ref.shape[0]
    step = pl.program_id(0)
    row = lax.broadcasted_iota(i32, (rows, 1), 0) + step * rows
    ids = jnp.where(row < count, row + base_ref[0], -1)
    columns = []
    for t_ref, first, second, begun in ((ty_ref, a_ref, b_ref, l_ref), (tx_ref, c_ref, d_ref, r_ref)):
        total = begun[...]
        for ref, low in ((first, 2 * PAD), (second, 2 * PAD + PAD // 2)):
            hit = (ids == t_ref[:, low : low + PAD // 2]).astype(bf16)
            total = total + mm(hit, ref[...])
        columns.append(total)
    total = jnp.concatenate(columns, axis=1) + h_ref[...].astype(f32)
    out_ref[...] = total
    total = jnp.where(row < count, total, 0.0)
    square = jnp.sum(total * total, axis=0, keepdims=True)
    square = jnp.broadcast_to(jnp.sum(square, axis=1, keepdims=True), (8, 128))
    top = lax.broadcasted_iota(i32, (8, 128), 0) < 4

    @pl.when(step == 0)
    def _():
        sum_ref[...] = m_ref[...] + jnp.where(top, square, 0.0)

    @pl.when(step > 0)
    def _():
        sum_ref[...] += jnp.where(top, square, 0.0)


def embed_end(count, base, tokens, halves, begun, head_part, sums, rows=256):
    return pl.pallas_call(
        functools.partial(embed_end_kernel, count),
        grid=(PAD // rows,),
        in_specs=[SCALARS]
        + [fixed(t.shape) for t in tokens]
        + [fixed(half.shape) for half in halves]
        + [pl.BlockSpec((rows, HALF), lambda i: (i, 0))] * 2
        + [pl.BlockSpec((rows, D), lambda i: (i, 0)), fixed((8, 128))],
        out_specs=[pl.BlockSpec((rows, D), lambda i: (i, 0)), whole((8, 128))],
        out_shape=[jax.ShapeDtypeStruct((PAD, D), f32), jax.ShapeDtypeStruct((8, 128), f32)],
        compiler_params=kernel_params(24),
        cost_estimate=work(4.5),
        name="embed_end",
    )(base, *tokens, *halves, *begun, head_part, sums)


def rows_grad_kernel(c_ref, o_ref, out_ref, square_ref):
    ffx = c_ref.shape[2] - 3 * HW
    parts = [c_ref[x, :, s * HW : (s + 1) * HW] for s in range(3) for x in range(NX)]
    parts += [o_ref[...]] + [c_ref[x, :, 3 * HW : 3 * HW + ffx] for x in range(NX)]
    total = jnp.concatenate(parts, axis=1)
    out_ref[...] = total
    square_ref[...] = jnp.sum(total * total, axis=0, keepdims=True)


def rows_grad(cols, out):
    rows, width = cols.shape[1], NX * cols.shape[2] + D
    return pl.pallas_call(
        rows_grad_kernel,
        grid=(1,),
        in_specs=[fixed(cols.shape), fixed(out.shape)],
        out_specs=[whole((rows, width)), whole((1, width))],
        out_shape=[
            jax.ShapeDtypeStruct((rows, width), f32),
            jax.ShapeDtypeStruct((1, width), f32),
        ],
        compiler_params=kernel_params(12),
        cost_estimate=work(1),
        name="rows_grad",
    )(cols, out)


def adam(start, gradient, moment, square, step_rate):
    moment_new = BETA_ONE * moment + (1.0 - BETA_ONE) * gradient
    square_new = BETA_TWO * square + (1.0 - BETA_TWO) * gradient * gradient
    fixed_moment = moment_new / (1.0 - BETA_ONE**STEP)
    fixed_square = square_new / (1.0 - BETA_TWO**STEP)
    moved = start - step_rate * (fixed_moment / (jnp.sqrt(fixed_square) + ADAM_EPS))
    return (moved, moment_new, square_new)


def per_device(
    token_ids,
    targets,
    segments,
    domains,
    embedding,
    w_rows,
    w_down,
    norm_gains,
    first_embed,
    first_rows,
    first_down,
    first_gains,
    second_embed,
    second_rows,
    second_down,
    second_gains,
    delta_embed,
    delta_rows,
    delta_down,
    delta_gains,
    outer_embed,
    outer_rows,
    outer_down,
    outer_gains,
):
    xi, yi, zi = (lax.axis_index(axis) for axis in ("x", "y", "z"))
    at = jnp.stack([xi, yi, zi])
    mine = (xi * NY + yi) * NZ + zi
    count = embedding.shape[1]
    rows_in = w_rows.shape[1]
    shards = NX * NY * NZ
    ffx = w_down.shape[1] * shards // NX
    back = jnp.arange(4, dtype=i32)
    bases_x = ((back * NY + yi) * NZ + zi) * count
    bases_y = ((xi * NY + (yi - back) % NY) * NZ + zi) * count
    key_bases = (
        (((xi - back[None, :]) % NX) * NY + (yi - back[:, None]) % NY) * PIECE
    ).reshape(-1)

    own = jnp.pad(embedding[0].astype(bf16), ((0, PAD - count), (0, 0)))
    table = lax.all_gather(own, "x", axis=0, tiled=True)

    rows_low = w_rows[0].astype(bf16)
    down_low = w_down[0].astype(bf16)

    def by_x(start_col, width):
        block = rows_low[:, start_col : start_col + NX * width]
        return jnp.transpose(block.reshape(rows_in, NX, width), (1, 0, 2))

    def pair_z(value):
        other = shift(value, "z", 1)
        return jnp.where(zi == 0, jnp.stack([value, other]), jnp.stack([other, value]))

    def whole_rows(value):
        return jnp.transpose(value, (2, 0, 1, 3, 4)).reshape(D, -1)

    gain_cols = norm_gains.shape[2]
    info = jnp.concatenate([token_ids[0], targets[0], segments[0], domains[0]], axis=0)
    gains_low = jnp.pad(norm_gains[0].astype(bf16), ((0, 5), (0, 0)))
    info = jnp.concatenate([(info // 256).astype(bf16), (info % 256).astype(bf16), gains_low], axis=1)
    info = jnp.pad(info, ((0, 0), (0, 3 * HW - info.shape[1])))
    cols = [by_x(0, HW), by_x(D, HW), by_x(2 * D, HW), by_x(4 * D, ffx)]
    cols = jnp.concatenate(cols, axis=2)
    info = jnp.pad(info, ((0, 0), (0, ffx)))
    cols = jnp.concatenate([cols, jnp.broadcast_to(info, (NX,) + info.shape)], axis=1)
    cols = lax.all_to_all(cols, "x", 0, 0, tiled=True)
    lines = cols.shape[1]
    early = cols[:, :, : 3 * HW].reshape(NX * lines, 3 * HW)
    late = jnp.concatenate(
        [
            cols[:, :rows_in, 3 * HW :].reshape(NX * rows_in, ffx),
            down_low,
            rows_low[:, 3 * D : 4 * D],
        ],
        axis=0,
    )
    early, late = pair_z(early), pair_z(late)
    early = order_y(at, gather_rel(early, "y"))
    late = order_y(at, gather_rel(late, "y"))
    cols = early.reshape(NY, NZ, NX, lines, 3 * HW)
    w_qkv = whole_rows(cols[:, :, :, :rows_in])
    split = NX * rows_in
    w_up = whole_rows(late[:, :, :split].reshape(NY, NZ, NX, rows_in, ffx))
    w_dn = late[:, :, split : split + down_low.shape[0]].reshape(ffx, D)
    w_out = late[:, :, split + down_low.shape[0] :].reshape(HW, D)
    info = cols[:, :, :, rows_in:, : 128 + gain_cols].astype(f32)
    gain = info[:, :, :, :3, 128:]
    gain = jnp.transpose(gain, (3, 2, 0, 1, 4)).reshape(3, D)
    frequency = jnp.exp(jnp.arange(HD // 2, dtype=f32) * (-math.log(10000.0) / (HD // 2)))
    frequency = jnp.broadcast_to(frequency[:, None], (HD // 2, 128))
    columns, lists, places, tokens_y, tokens_x, counts, cosine, sine = prep(
        at, info[..., :128].reshape(shards, lines - rows_in, 128), key_bases, frequency
    )
    counts = counts[:NDOM, 0]
    targets_row = lists[:, :PAD].astype(i32)

    found = lookup(bases_x, columns, 0, table)
    w_outs = lax.all_gather(tie(w_out, table), "x")
    wanted = lookup(tie(bases_x, found), columns, 2, table)
    parts = scatter_rel([found[k * NZ * PIECE : (k + 1) * NZ * PIECE] for k in range(NY)], "y")
    parts, wanted = lax.optimization_barrier((parts, wanted))
    found = sum32(parts).astype(bf16)
    x0_own = sum32(scatter_rel([found[:PIECE], found[PIECE:]], "z"))
    wanted = lax.psum_scatter(wanted, "y", scatter_dimension=0, tiled=True)
    x0_pieces = gather_rel(x0_own.astype(bf16), "x")

    x0, a, q, kv = qkv(x0_pieces, gain[0:1], w_qkv, cosine, sine)
    kvs = gather_rel(kv, "y")
    o, lse_q = attend(key_bases, q, kvs, places)
    os = gather_rel(o, "x")
    x1 = x0.astype(f32)
    for s, heads in enumerate(os):
        pieces = [heads[((j - s) % NX) * PIECE : ((j - s) % NX + 1) * PIECE] for j in range(NX)]
        heads = jnp.concatenate(pieces, axis=0) if s else heads
        x1 = x1 + mm(heads, lax.dynamic_index_in_dim(w_outs, (xi - s) % NX, 0, False))

    b = rms_norm(x1, gain[1]).astype(bf16)
    up = mm(b, w_up)
    hmid = jax.nn.gelu(up).astype(bf16)
    part = mm(hmid, w_dn).astype(bf16).reshape(NX, PIECE, D)
    parts = scatter_rel([part[k] for k in range(NX)], "x")
    target_rows = scatter_rel([wanted[:PIECE], wanted[PIECE:]], "z")
    parts, target_rows = lax.optimization_barrier((parts, target_rows))
    x2 = x1[:PIECE] + sum32(parts)
    hf = rms_norm(x2, gain[2]).astype(bf16)

    states = gather_rel(jnp.concatenate(gather_rel(hf, "z"), axis=0), "y")
    *rest_sum, stats = head(count, bases_x, states, table, columns)
    stats = lax.all_to_all(stats, ("y", "z"), 0, 0, tiled=True)
    terms = [rest_sum[0]]
    for index in range(1, NY * NZ):
        ky, kz = index // NZ, index % NZ
        perm = [
            (y * NZ + z, ((y - ky) % NY) * NZ + (z - kz) % NZ)
            for y in range(NY)
            for z in range(NZ)
        ]
        terms.append(lax.ppermute(rest_sum[index], ("y", "z"), perm))
    stats, scales, sums_own = merge(at, stats, lists)
    def head_grad(chunk, after, before=None):
        return table_grad(
            chunk, tie(bases_x, after), table, states, targets_row, stats, before
        )

    from_head = head_grad(0, stats)
    terms, from_head = lax.optimization_barrier((terms, from_head))
    d_hf = -scales[:, NY * NZ : NY * NZ + 1] * sum32(target_rows)
    for index, term in enumerate(terms):
        d_hf = d_hf + scales[:, index : index + 1] * term.astype(f32)

    dx2, gain_two = rms_back(x2, gain[2], d_hf)
    dx2_low = dx2.astype(bf16)
    g2 = gather_rel(dx2_low, "x")
    from_head = head_grad(1, dx2_low, from_head)
    g2, from_head = lax.optimization_barrier((g2, from_head))
    g2 = jnp.concatenate(g2, axis=0)
    unused, pull_gelu = jax.vjp(jax.nn.gelu, up)
    d_up = pull_gelu(mm_nt(g2, w_dn))[0].astype(bf16)
    part = mm_nt(d_up, w_up).astype(bf16)
    d_b = scatter_rel([part[k * PIECE : (k + 1) * PIECE] for k in range(NX)], "x")

    def to_yz(value):
        value = value.astype(bf16).reshape(NX, NY * NZ, rows_in, value.shape[1])
        return jnp.transpose(value, (1, 0, 2, 3)).reshape(NY * NZ, NX * rows_in, -1)

    def scatter_yz(value):
        value = lax.all_to_all(value, ("y", "z"), 0, 0, tiled=True)
        return sum32([value[k] for k in range(NY * NZ)])

    g2_low, d_up_low = tie((g2, d_up), part)
    ffn_grad = jnp.concatenate(
        [
            to_yz(mm_tn(b, d_up_low)),
            mm_tn(hmid, g2_low).astype(bf16).reshape(NY * NZ, -1, D),
        ],
        axis=1,
    )
    from_head = head_grad(2, part, from_head)
    d_b, ffn_grad, from_head = lax.optimization_barrier((d_b, ffn_grad, from_head))
    d_b = sum32(d_b)

    d_norm, gain_one = rms_back(x1[:PIECE], gain[1], d_b)
    dx1 = dx2 + d_norm
    dx1_low = dx1.astype(bf16)
    g1 = gather_rel(dx1_low, "x")
    from_head = head_grad(3, dx1_low, from_head)
    g1, from_head = lax.optimization_barrier((g1, from_head))
    ffn_grad = scatter_yz(tie(ffn_grad, g1))
    from_head = lax.psum_scatter(from_head, "x", scatter_dimension=0, tiled=True)
    dq, *dkvs = attend_back(key_bases, q, kvs, places, lse_q, g1, w_out)
    g1_low = jnp.concatenate(tie(g1, dkvs[0]), axis=0)
    out_grad = mm_tn(o, g1_low).astype(bf16)
    dkvs = scatter_rel(dkvs, "y")
    dkvs, out_grad, ffn_grad = lax.optimization_barrier((dkvs, out_grad, ffn_grad))
    d_mixed, part = qkv_back(dq, dkvs, cosine, sine, w_qkv)
    d_a = scatter_rel([part[k * PIECE : (k + 1) * PIECE] for k in range(NX)], "x")
    qkv_grad = to_yz(mm_tn(a, tie(d_mixed, part)))
    d_a, qkv_grad = lax.optimization_barrier((d_a, qkv_grad))
    d_norm, gain_zero = rms_back(x0_own, gain[0], sum32(d_a))
    gz = (dx1 + d_norm).astype(bf16)

    gz_pair = jnp.concatenate(gather_rel(gz, "z"), axis=0)
    by_y = jnp.concatenate(gather_rel(gz_pair[:, :HALF], "x"), axis=0)
    by_x = jnp.concatenate(gather_rel(gz_pair[:, HALF:], "y"), axis=0)
    by_y, by_x = gather_ring(by_y, "y"), gather_ring(by_x, "x")
    base_own = (mine * count).reshape(1)

    def two_terms(value):
        high = lax.reduce_precision(value, 8, 7)
        return jnp.concatenate([high, value - high], axis=1)

    def one_term(value):
        width = value.shape[1] // 2
        return value[:, :width] + value[:, width:]

    gains_grad = jnp.stack(tie([gain_zero, gain_one, gain_two], gz))
    gains_grad = gains_grad.reshape(3, NX, NY * NZ, gain_cols).transpose(2, 1, 0, 3)
    gains_grad = two_terms(gains_grad.reshape(NY * NZ, -1))
    gains_grad = jnp.pad(gains_grad[:, None, :], ((0, 0), (0, 15), (0, 0)))
    split = NX * rows_in
    qkv_grad = jnp.concatenate(
        [qkv_grad, out_grad.reshape(NY * NZ, -1, 3 * HW), gains_grad.astype(bf16)], axis=1
    )
    qkv_grad = scatter_yz(tie(qkv_grad, gz_pair))
    gains_grad = two_terms(one_term(qkv_grad[-16:-15]).reshape(NX, -1))
    gains_grad = jnp.pad(
        gains_grad[:, None, :], ((0, 0), (0, 7), (0, 3 * HW + ffx - gains_grad.shape[1]))
    )
    cols_grad = jnp.concatenate(
        [
            qkv_grad[:split].reshape(NX, rows_in, 3 * HW),
            ffn_grad[:split].reshape(NX, rows_in, ffx),
        ],
        axis=2,
    )
    cols_grad = jnp.concatenate([cols_grad, gains_grad], axis=1).astype(bf16)
    cols_grad = lax.all_to_all(cols_grad, "x", 0, 0, tiled=True).astype(f32)
    rows_own, square_rows = rows_grad(
        cols_grad[:, :rows_in], qkv_grad[split:-16].reshape(rows_in, D)
    )
    down_own = ffn_grad[split:]
    gains_own = jnp.sum(cols_grad[:, rows_in, : 6 * gain_cols], axis=0, keepdims=True)
    gains_own = one_term(gains_own).reshape(3, gain_cols)

    lead = delta_down.shape[1]
    delta_tail = jnp.concatenate(
        [delta_down[0], jnp.pad(delta_gains[0], ((0, 5), (0, D - gain_cols)))], axis=0
    )
    summed = lax.psum((delta_embed[0], delta_rows[0], delta_tail), ("zh", "c"))
    summed = tie(summed, gz_pair)
    summed = (summed[0], summed[1], summed[2][:lead], summed[2][lead : lead + 3, :gain_cols])
    group_count = lax.axis_size("zh") * lax.axis_size("c")
    weights_now = (embedding[0], w_rows[0], w_down[0], norm_gains[0])
    outers = (outer_embed, outer_rows, outer_down, outer_gains)
    means = [part_sum / group_count for part_sum in summed]
    momenta = [OUTER_MU * outer + mean for outer, mean in zip(outers, means)]
    starts = []
    for kind_index in range(4):
        shrink = 1.0 - (0.0 if kind_index == 3 else RATE * DECAY)
        starts.append(
            shrink * weights_now[kind_index]
            - OUTER_RATE * (means[kind_index] + OUTER_MU * momenta[kind_index])
        )

    squares = jnp.sum(square_rows) + jnp.sum(down_own * down_own) + jnp.sum(gains_own * gains_own)
    sums = jnp.concatenate(
        [jnp.broadcast_to(squares, (4, 128)), jnp.broadcast_to(sums_own, (4, 128))], axis=0
    )
    begun = [
        embed_start(count, base_own, tokens, [parts[0], parts[1], parts[4]])
        for tokens, parts in ((tokens_y, by_y), (tokens_x, by_x))
    ]
    halves, begun, sums, means, momenta, starts = lax.optimization_barrier(
        (by_y[2:4] + by_x[2:4], begun, sums, means, momenta, starts)
    )
    table, totals = embed_end(
        count, base_own, (tokens_y, tokens_x), halves, begun, from_head, sums
    )

    gradients = (table[:count], rows_own, down_own, gains_own)
    totals = all_sum(totals)
    domain_sums = totals[4, :NDOM]
    size_now = jnp.sqrt(totals[0, 0])
    factor = jnp.minimum(1.0, CLIP / size_now)

    firsts = (first_embed[0], first_rows[0], first_down[0], first_gains[0])
    seconds = (second_embed[0], second_rows[0], second_down[0], second_gains[0])
    new_items, moment_items, square_items = ([], [], [])
    for kind_index in range(4):
        moved, moment_new, square_new = adam(
            starts[kind_index],
            gradients[kind_index] * factor,
            firsts[kind_index],
            seconds[kind_index],
            GAIN_RATE if kind_index == 3 else RATE,
        )
        new_items.append(moved[None])
        moment_items.append(moment_new[None])
        square_items.append(square_new[None])
    return (
        domain_sums[None],
        counts[None],
        size_now.reshape(1),
        *new_items,
        *moment_items,
        *square_items,
        *means,
        *momenta,
    )


def solution(mesh):
    groups = mesh.shape["group"]
    high = 2 if groups % 2 == 0 else 1
    fine = Mesh(
        mesh.devices.reshape(high, groups // high, NX, NY, NZ), ("zh", "c", "x", "y", "z")
    )
    group, blk = ("zh", "c"), ("x", "y", "z")
    tokens = P(group, None, blk)
    rows = P(group, blk, None)
    gains = P(group, None, blk)
    kind = (rows, rows, rows, gains)
    shared = (P(blk, None), P(blk, None), P(blk, None), P(None, blk))
    return jax.shard_map(
        per_device,
        mesh=fine,
        in_specs=(tokens,) * 4 + kind * 4 + shared,
        out_specs=(P(group, None), P(group, None), P(group)) + kind * 3 + shared * 2,
        check_vma=False,
    )
```

```python
import functools
import math

import jax
import jax.numpy as jnp
from jax import lax
from jax.experimental import pallas as pl
from jax.experimental.pallas import tpu as pltpu
from jax.sharding import Mesh, PartitionSpec as P

D = 768
HD = 64
NDOM = 4
STEP = 10
SEGS = 8
PAD = 1024
HALF = D // 2

EPS = 1e-06
BETA_ONE = 0.9
BETA_TWO = 0.95
ADAM_EPS = 1e-08
DECAY = 0.1
RATE = 0.02
GAIN_RATE = 0.2
CLIP = 0.05
OUTER_RATE = 0.7
OUTER_MU = 0.9

NX, NY, NZ = 4, 4, 2
SIZE = {"x": NX, "y": NY, "z": NZ}
PIECE = 128
BLOCK = NX * PIECE
HEADS = D // HD // NX
HW = HEADS * HD
NEG = -1e30

bf16, f32, i32 = jnp.bfloat16, jnp.float32, jnp.int32


def shift(value, axis, step):
    size = SIZE[axis]
    return lax.ppermute(value, axis, [(i, (i + step) % size) for i in range(size)])


def gather_rel(value, axis):
    return [value] + [shift(value, axis, k) for k in range(1, SIZE[axis])]


def scatter_rel(parts, axis):
    return [parts[0]] + [shift(parts[k], axis, -k) for k in range(1, SIZE[axis])]


def gather_ring(value, axis):
    half = value.shape[0] // 2
    before, after = shift(value, axis, 1), shift(value, axis, -1)
    first, second = shift(before[:half], axis, 1), shift(after[half:], axis, -1)
    return [value, before, first, second, after]


def spans(parts):
    start, found = 0, []
    for part in parts:
        found.append((start, start + part.shape[0]))
        start += part.shape[0]
    return found


def sum32(parts):
    total = parts[0].astype(f32)
    for part in parts[1:]:
        total = total + part.astype(f32)
    return total


def all_sum(value):
    for axis in ("z", "y", "x"):
        value = functools.reduce(jnp.add, gather_rel(value, axis))
    return value


def mm(a, b):
    return jnp.dot(a, b, preferred_element_type=f32)


def mm_nt(a, b):
    return lax.dot_general(a, b, (((1,), (1,)), ((), ())), preferred_element_type=f32)


def mm_tn(a, b):
    return lax.dot_general(a, b, (((0,), (0,)), ((), ())), preferred_element_type=f32)


def rms_norm(values, scales):
    return values * lax.rsqrt(jnp.mean(values * values, axis=-1, keepdims=True) + EPS) * scales


def rms_back(values, scales, grad):
    inverse = lax.rsqrt(jnp.mean(values * values, axis=-1, keepdims=True) + EPS)
    unit = values * inverse
    scaled = grad * scales
    grad_values = inverse * (scaled - unit * jnp.mean(scaled * unit, axis=-1, keepdims=True))
    return grad_values, jnp.sum(grad * unit, axis=0)


def tie(values, after):
    return lax.optimization_barrier((values, after))[0]


def turn_lanes(values):
    half = HD // 2
    parts = []
    for start in range(0, values.shape[1], HD):
        parts += [values[:, start + half : start + HD], values[:, start : start + half]]
    return jnp.concatenate(parts, axis=1)


def whole(shape):
    return pl.BlockSpec(shape, lambda *_: (0,) * len(shape))


def fixed(shape):
    return pl.BlockSpec(shape, lambda *_: (0,) * len(shape), pipeline_mode=pl.Buffered(1))


def kernel_params(mib):
    return pltpu.CompilerParams(vmem_limit_bytes=mib * 2**20)


def work(micros):
    return pl.CostEstimate(
        flops=int(micros * 1e9), bytes_accessed=int(micros * 3e6), transcendentals=0
    )


SCALARS = pl.BlockSpec(memory_space=pltpu.SMEM)
ANYWHERE = pl.BlockSpec(memory_space=pl.ANY)


def prep_kernel(
    at_ref, info_ref, base_ref, freq_ref, cols_ref, lists_ref, rows_ref, by_y_ref, by_x_ref, misc_ref, cos_ref, sin_ref
):
    xi, yi, first = at_ref[0], at_ref[1], at_ref[2] == 0

    def tile(y, x):
        halves = []
        for z in range(NZ):
            block = info_ref[(y * NZ + z) * NX + x]
            halves.append(block[:, :64] * 256.0 + block[:, 64:128])
        return jnp.concatenate(halves, axis=1)

    def row(block, kind, other):
        low, high = block[2 * kind : 2 * kind + 1], block[2 * kind + 1 : 2 * kind + 2]
        return jnp.where(first, high, low) if other else jnp.where(first, low, high)

    def lanes(parts):
        return jnp.concatenate(parts, axis=1)

    def pairs(blocks, kind):
        return [row(block, kind, zr) for block in blocks for zr in range(NZ)]

    near = [
        [tile(lax.rem(yi + NY - yb, NY), lax.rem(xi + NX - xb, NX)) for xb in range(NX)]
        for yb in range(NY)
    ]
    flat = [block for line in near for block in line]
    over_y, over_x = [line[0] for line in near], near[0]
    counts = []
    for d in range(NDOM):
        hits = sum(jnp.where(r == float(d), 1.0, 0.0) for r in pairs(flat, 3))
        counts.append(jnp.sum(hits, axis=1, keepdims=True))
    domain = lanes(pairs(over_y, 3))
    weight = jnp.zeros_like(domain)
    for d in range(NDOM):
        weight = jnp.where(domain == float(d), 1.0 / (NDOM * counts[d]), weight)
    lists_ref[...] = lanes(pairs(over_y, 1) + [domain, weight])
    along_y = [tile(y, xi) for y in range(NY)]
    columns = zip(
        pairs(over_y, 0), pairs(over_y, 1), pairs(along_y, 1)
    )
    for k, parts in enumerate(columns):
        square = jnp.concatenate(
            list(parts) + [jnp.zeros((PIECE - len(parts), PIECE), f32)], axis=0
        )
        cols_ref[k * PIECE : (k + 1) * PIECE, :] = jnp.transpose(square).astype(i32)
    seg, seg_own = lanes([row(b, 2, 0) for b in flat]), lanes([row(b, 2, 0) for b in over_x])
    lane = lax.broadcasted_iota(i32, (1, PIECE), 1)
    place = lanes([lane + base_ref[xb] for xb in range(NX)])
    start = jnp.zeros((1, BLOCK), i32)
    for s in range(1, SEGS):
        before = jnp.sum(jnp.where(seg < float(s), 1.0, 0.0), axis=1, keepdims=True)
        start = jnp.where(seg_own == float(s), before.astype(i32), start)
    rows_ref[...] = jnp.concatenate(
        [place, place - start, jnp.zeros((6, BLOCK), i32)], axis=0
    )
    by_x = [tile(lax.rem(yi + NY - yb, NY), x) for x in range(NX) for yb in range(NY)]
    by_y_ref[...] = lanes(pairs(flat, 0)).astype(i32)
    by_x_ref[...] = lanes(pairs(by_x, 0)).astype(i32)
    misc_ref[...] = jnp.concatenate(
        [jnp.broadcast_to(c, (1, 128)) for c in counts] + [jnp.zeros((4, 128), f32)], axis=0
    )
    angle = (place - start).astype(f32) * freq_ref[:, :1]
    cosine, sine = jnp.cos(angle), jnp.sin(angle)
    cos_ref[...] = jnp.transpose(jnp.concatenate([cosine] * 4, axis=0))
    sin_ref[...] = jnp.transpose(jnp.concatenate([-sine, sine] * 2, axis=0))


def prep(at, info, bases, frequency):
    shapes = [
        ((PAD, 128), i32),
        ((1, 3 * PAD), f32),
        ((8, BLOCK), i32),
        ((1, 4 * PAD), i32),
        ((1, 4 * PAD), i32),
        ((8, 128), f32),
        ((BLOCK, 128), f32),
        ((BLOCK, 128), f32),
    ]
    return pl.pallas_call(
        prep_kernel,
        in_specs=[SCALARS, fixed(info.shape), SCALARS, fixed(frequency.shape)],
        out_specs=[whole(s) for s, _ in shapes],
        out_shape=[jax.ShapeDtypeStruct(s, t) for s, t in shapes],
        grid=(1,),
        compiler_params=kernel_params(12),
        cost_estimate=work(1.4),
        name="prep",
    )(at, info, bases, frequency)


def order_kernel(at_ref, a_ref, b_ref, c_ref, d_ref, out_ref, sem):
    copies = [
        pltpu.make_async_copy(ref, out_ref.at[lax.rem(at_ref[1] + NY - k, NY)], sem.at[k])
        for k, ref in enumerate((a_ref, b_ref, c_ref, d_ref))
    ]
    for copy in copies:
        copy.start()
    for copy in copies:
        copy.wait()


def order_y(at, parts):
    return pl.pallas_call(
        order_kernel,
        in_specs=[SCALARS] + [ANYWHERE] * NY,
        out_specs=ANYWHERE,
        out_shape=jax.ShapeDtypeStruct((NY,) + parts[0].shape, parts[0].dtype),
        scratch_shapes=[pltpu.SemaphoreType.DMA((NY,))],
        compiler_params=kernel_params(4),
        cost_estimate=work(2),
        name="order_y",
    )(at, *parts)


def lookup_kernel(column, base_ref, t_ref, table_ref, out_ref):
    tokens = t_ref[:, column : column + 1]
    total = None
    for k in range(NX):
        ids = lax.broadcasted_iota(i32, (1, PAD), 1) + base_ref[k]
        hit = (tokens == ids).astype(bf16)
        term = mm(hit, table_ref[k * PAD : (k + 1) * PAD, :])
        total = term if total is None else total + term
    out_ref[...] = total.astype(bf16)


def lookup(bases, tokens, column, table, rows=1024):
    n = tokens.shape[0]
    return pl.pallas_call(
        functools.partial(lookup_kernel, column),
        grid=(n // rows,),
        in_specs=[
            SCALARS,
            pl.BlockSpec((rows, 128), lambda i: (i, 0)),
            fixed(table.shape),
        ],
        out_specs=pl.BlockSpec((rows, D), lambda i: (i, 0)),
        out_shape=jax.ShapeDtypeStruct((n, D), bf16),
        compiler_params=kernel_params(28),
        cost_estimate=work(10),
        name="lookup",
    )(bases, tokens, table)


def qkv_kernel(
    a_ref, b_ref, c_ref, d_ref, g_ref, w_ref, cos_ref, sin_ref, x_ref, n_ref, q_ref, kv_ref
):
    for k, ref in enumerate((a_ref, b_ref, c_ref, d_ref)):
        rows = slice(k * PIECE, (k + 1) * PIECE)
        x_ref[rows, :] = ref[...]
        normed = rms_norm(ref[...].astype(f32), g_ref[...]).astype(bf16)
        n_ref[rows, :] = normed
        mixed = mm(normed, w_ref[...])
        turned = mixed[:, : 2 * HW]
        cosine = jnp.concatenate([cos_ref[rows, :]] * 3, axis=1)
        sine = jnp.concatenate([sin_ref[rows, :]] * 3, axis=1)
        turned = turned * cosine + turn_lanes(turned) * sine
        q_ref[rows, :] = turned[:, :HW].astype(bf16)
        kv_ref[rows, :] = jnp.concatenate([turned[:, HW:], mixed[:, 2 * HW :]], axis=1).astype(
            bf16
        )


def qkv(pieces, gain, weights, cosine, sine):
    shapes = [(BLOCK, D), (BLOCK, D), (BLOCK, HW), (BLOCK, 2 * HW)]
    return pl.pallas_call(
        qkv_kernel,
        grid=(1,),
        in_specs=[fixed((PIECE, D))] * 4
        + [fixed((1, D)), fixed(weights.shape), fixed(cosine.shape), fixed(sine.shape)],
        out_specs=[whole(s) for s in shapes],
        out_shape=[jax.ShapeDtypeStruct(s, bf16) for s in shapes],
        compiler_params=kernel_params(16),
        cost_estimate=work(2.3),
        name="qkv",
    )(*pieces, gain, weights, cosine, sine)


def qkv_back_kernel(
    dq_ref, a_ref, b_ref, c_ref, d_ref, cos_ref, sin_ref, w_ref, x_ref, mixed_ref, part_ref, gain_ref
):
    gain = None
    for k in range(NX):
        rows = slice(k * PIECE, (k + 1) * PIECE)
        dkv = sum32([ref[rows, :] for ref in (a_ref, b_ref, c_ref, d_ref)])
        turned = jnp.concatenate([dq_ref[rows, :], dkv[:, :HW]], axis=1)
        cosine = jnp.concatenate([cos_ref[rows, :]] * 3, axis=1)
        sine = jnp.concatenate([sin_ref[rows, :]] * 3, axis=1)
        raw = turned * cosine + turn_lanes(turned * sine)
        mixed = jnp.concatenate([raw, dkv[:, HW:]], axis=1).astype(bf16)
        mixed_ref[rows, :] = mixed
        part = mm_nt(mixed, w_ref[...])
        part_ref[rows, :] = part.astype(bf16)
        x = x_ref[rows, :].astype(f32)
        unit = x * lax.rsqrt(jnp.mean(x * x, axis=-1, keepdims=True) + EPS)
        share = jnp.sum(part * unit, axis=0, keepdims=True)
        gain = share if gain is None else gain + share
    gain_ref[...] = gain


def qkv_back(dq, dkvs, cosine, sine, weights, x0):
    shapes = [((BLOCK, 3 * HW), bf16), ((BLOCK, D), bf16), ((1, D), f32)]
    return pl.pallas_call(
        qkv_back_kernel,
        grid=(1,),
        in_specs=[fixed((BLOCK, HW))]
        + [fixed((BLOCK, 2 * HW))] * 4
        + [fixed(cosine.shape), fixed(sine.shape), fixed(weights.shape), fixed(x0.shape)],
        out_specs=[whole(s) for s, _ in shapes],
        out_shape=[jax.ShapeDtypeStruct(s, t) for s, t in shapes],
        compiler_params=kernel_params(16),
        cost_estimate=work(2),
        name="qkv_back",
    )(dq, *dkvs, cosine, sine, weights, x0)


def fill_bias(base_ref, rows_ref, bias_ref):
    query, reach = rows_ref[0:1, :], rows_ref[1:2, :]
    key = lax.broadcasted_iota(i32, (PIECE, BLOCK), 0)
    for j in range(NX * NY):
        back = (query - base_ref[j]) - key
        bias_ref[j * PIECE : (j + 1) * PIECE, :] = jnp.where(
            (back >= 0) & (back <= reach), 0.0, NEG
        )


def attend_kernel(
    base_ref, q_ref, a_ref, b_ref, c_ref, d_ref, rows_ref, o_ref, lse_ref, kv_ref, bias_ref
):
    pieces = (a_ref, b_ref, c_ref, d_ref)
    for ref, (low, high) in zip(pieces, spans(pieces)):
        kv_ref[low:high, :] = ref[...]
    fill_bias(base_ref, rows_ref, bias_ref)
    q = q_ref[...] * jnp.asarray(HD**-0.5, bf16)
    outs, tops = [], []
    for h in range(HEADS):
        a, b = h * HD, (h + 1) * HD
        scores = mm_nt(kv_ref[:, a:b], q[:, a:b]) + bias_ref[...]
        top = jnp.max(scores, axis=0, keepdims=True)
        weight = jnp.exp(scores - top)
        total = jnp.sum(weight, axis=0, keepdims=True)
        probs = (weight * (1.0 / total)).astype(bf16)
        outs.append(mm_tn(kv_ref[:, HW + a : HW + b], probs))
        tops.append(top + jnp.log(total))
    o_ref[...] = jnp.transpose(jnp.concatenate(outs, axis=0)).astype(bf16)
    lse_ref[...] = jnp.concatenate(tops + [jnp.zeros((8 - HEADS, BLOCK), f32)], axis=0)


def attend(bases, q, kvs, rows):
    keys = NY * BLOCK
    return pl.pallas_call(
        attend_kernel,
        grid=(1,),
        in_specs=[SCALARS, fixed((BLOCK, HW))]
        + [fixed(kv.shape) for kv in kvs]
        + [fixed((8, BLOCK))],
        out_specs=[whole((BLOCK, HW)), whole((8, BLOCK))],
        out_shape=[
            jax.ShapeDtypeStruct((BLOCK, HW), bf16),
            jax.ShapeDtypeStruct((8, BLOCK), f32),
        ],
        scratch_shapes=[pltpu.VMEM((keys, 2 * HW), bf16), pltpu.VMEM((keys, BLOCK), f32)],
        compiler_params=kernel_params(24),
        cost_estimate=work(8.5),
        name="attend",
    )(bases, q, *kvs, rows)


def attend_back_kernel(
    base_ref,
    q_ref,
    a_ref,
    b_ref,
    c_ref,
    d_ref,
    rows_ref,
    lse_ref,
    ga_ref,
    gb_ref,
    gc_ref,
    gd_ref,
    w_ref,
    dq_ref,
    da_ref,
    db_ref,
    dc_ref,
    dd_ref,
    kv_ref,
    bias_ref,
):
    pieces = (a_ref, b_ref, c_ref, d_ref)
    for ref, (low, high) in zip(pieces, spans(pieces)):
        kv_ref[low:high, :] = ref[...]
    fill_bias(base_ref, rows_ref, bias_ref)
    q = q_ref[...]
    grad = jnp.concatenate(
        [mm_nt(ref[...], w_ref[...]).astype(bf16) for ref in (ga_ref, gb_ref, gc_ref, gd_ref)],
        axis=0,
    )
    scaled = q * jnp.asarray(HD**-0.5, bf16)
    dqs, dks, dvs = [], [], []
    for h in range(HEADS):
        a, b = h * HD, (h + 1) * HD
        key = kv_ref[:, a:b]
        scores = mm_nt(key, scaled[:, a:b]) + bias_ref[...]
        probs = jnp.exp(scores - lse_ref[h : h + 1, :])
        dprobs = mm_nt(kv_ref[:, HW + a : HW + b], grad[:, a:b])
        both = probs * dprobs
        row = jnp.sum(both, axis=0, keepdims=True)
        dscores = ((both - probs * row) * HD**-0.5).astype(bf16)
        dqs.append(mm_tn(key, dscores))
        dks.append(mm(dscores, q[:, a:b]).astype(bf16))
        dvs.append(mm(probs.astype(bf16), grad[:, a:b]).astype(bf16))
    dq_ref[...] = jnp.transpose(jnp.concatenate(dqs, axis=0))
    for k, ref in enumerate((da_ref, db_ref, dc_ref, dd_ref)):
        rows = slice(k * BLOCK, (k + 1) * BLOCK)
        ref[...] = jnp.concatenate([part[rows] for part in dks + dvs], axis=1)


def attend_back(bases, q, kvs, rows, lse, grads, weights):
    keys = NY * BLOCK
    return pl.pallas_call(
        attend_back_kernel,
        grid=(1,),
        in_specs=[SCALARS, fixed((BLOCK, HW))]
        + [fixed(kv.shape) for kv in kvs]
        + [fixed((8, BLOCK)), fixed((8, BLOCK))]
        + [fixed((PIECE, D))] * 4
        + [fixed((HW, D))],
        out_specs=[whole((BLOCK, HW))] + [whole((BLOCK, 2 * HW))] * 4,
        out_shape=[jax.ShapeDtypeStruct((BLOCK, HW), f32)]
        + [jax.ShapeDtypeStruct((BLOCK, 2 * HW), bf16)] * 4,
        scratch_shapes=[pltpu.VMEM((keys, 2 * HW), bf16), pltpu.VMEM((keys, BLOCK), f32)],
        compiler_params=kernel_params(32),
        cost_estimate=work(13.5),
        name="attend_back",
    )(bases, q, *kvs, rows, lse, *grads, weights)


def head_kernel(count, many, base_ref, *refs):
    states, t_ref, far_ref = refs[:many], refs[many], refs[many + 1]
    outs = refs[many + 2 : many + 2 + NY * NZ]
    stats_ref, h_ref, table, sem = refs[many + 2 + NY * NZ :]
    copy = pltpu.make_async_copy(far_ref, table, sem)
    copy.start()
    for ref, (low, high) in zip(states, spans(states)):
        h_ref[low:high, :] = ref[...]
    copy.wait()
    targets = t_ref[:, 1:2]
    states = h_ref[...]
    column = lax.broadcasted_iota(i32, (1, PAD), 1)
    top = None
    for k in range(NX):
        block = table[k * PAD : (k + 1) * PAD, :]
        logits = mm_nt(states, block)
        cut = count // 128 * 128
        spare = jnp.where(column[:, cut:] < count, 0.0, NEG)
        logits = jnp.concatenate([logits[:, :cut], logits[:, cut:] + spare], axis=1)
        hit = targets == jnp.where(column < count, column + base_ref[k], -1)
        here = jnp.max(logits, axis=1, keepdims=True)
        found = jnp.max(jnp.where(hit, logits, NEG), axis=1, keepdims=True)
        if top is None:
            top, pick = here, found
            weight = jnp.where(hit, 0.0, jnp.exp(logits - top))
            rest = jnp.sum(weight, axis=1, keepdims=True)
            total = mm(weight.astype(bf16), block)
        else:
            higher = jnp.maximum(top, here)
            scale = jnp.exp(top - higher)
            pick = jnp.maximum(pick, found)
            weight = jnp.where(hit, 0.0, jnp.exp(logits - higher))
            rest = rest * scale + jnp.sum(weight, axis=1, keepdims=True)
            total = total * scale + mm(weight.astype(bf16), block)
            top = higher
    for k, out_ref in enumerate(outs):
        out_ref[...] = total[k * PIECE : (k + 1) * PIECE].astype(bf16)
    stats = jnp.concatenate([top, rest, pick, jnp.zeros((top.shape[0], 125), f32)], axis=1)
    stats = jnp.transpose(stats)[:8, :]
    for k in range(NY * NZ):
        stats_ref[k] = stats


def head(count, bases, states, table, targets):
    n = NY * NZ * PIECE
    return pl.pallas_call(
        functools.partial(head_kernel, count, len(states)),
        grid=(1,),
        in_specs=[SCALARS]
        + [fixed(part.shape) for part in states]
        + [fixed((n, 128)), ANYWHERE],
        out_specs=[whole((PIECE, D))] * (NY * NZ) + [whole((NY * NZ, 8, n))],
        out_shape=[jax.ShapeDtypeStruct((PIECE, D), bf16)] * (NY * NZ)
        + [jax.ShapeDtypeStruct((NY * NZ, 8, n), f32)],
        scratch_shapes=[
            pltpu.VMEM((n, D), bf16),
            pltpu.VMEM((NX * PAD, D), bf16),
            pltpu.SemaphoreType.DMA,
        ],
        compiler_params=kernel_params(38),
        cost_estimate=work(20),
        name="head",
    )(bases, *states, targets, table)


def merge_kernel(at_ref, stats_ref, lists_ref, rows_ref, cols_ref, sums_ref):
    n = NY * NZ * PIECE

    def ordered(values, k, kz):
        parts = []
        for l in range(NY):
            for zr in range(NZ):
                at = (((l - k) % NY) * NZ + (zr - kz) % NZ) * PIECE
                parts.append(values[:, at : at + PIECE])
        return jnp.concatenate(parts, axis=1)

    shards = {}
    for k in range(NY):
        for kz in range(NZ):
            y, z = lax.rem(at_ref[1] + NY - k, NY), lax.rem(at_ref[2] + NZ - kz, NZ)
            shards[k, kz] = stats_ref[y * NZ + z]
    shards = {key: ordered(values, *key) for key, values in shards.items()}
    domain, weight = lists_ref[:, n : 2 * n], lists_ref[:, 2 * n : 3 * n]
    top = functools.reduce(jnp.maximum, [s[0:1] for s in shards.values()])
    rest = sum(s[1:2] * jnp.exp(s[0:1] - top) for s in shards.values())
    pick = functools.reduce(jnp.maximum, [s[2:3] for s in shards.values()])
    total = rest + jnp.exp(pick - top)
    lse = top + jnp.log(total)
    missing = weight * (rest / total)
    rows_ref[...] = jnp.concatenate([lse, weight, -missing, jnp.zeros((5, n), f32)], axis=0)
    mine = slice(0, PIECE)
    scales = []
    for ky in range(NY):
        for kz in range(NZ):
            stats = shards[(-ky) % NY, kz]
            scales.append(weight[:, mine] * jnp.exp(stats[0:1, mine] - lse[:, mine]))
    scales += [missing[:, mine], jnp.zeros((128 - len(scales) - 1, PIECE), f32)]
    cols_ref[...] = jnp.transpose(jnp.concatenate(scales, axis=0))
    loss = lse[:, mine] - pick[:, mine]
    lane = lax.broadcasted_iota(i32, (1, 128), 1)
    sums = jnp.zeros((1, 128), f32)
    for d in range(NDOM):
        part = jnp.sum(jnp.where(domain[:, mine] == float(d), loss, 0.0), axis=1, keepdims=True)
        sums = jnp.where(lane == d, part, sums)
    sums_ref[...] = sums


def merge(at, stats, lists):
    n = NY * NZ * PIECE
    return pl.pallas_call(
        merge_kernel,
        grid=(1,),
        in_specs=[SCALARS, fixed(stats.shape), fixed(lists.shape)],
        out_specs=[whole((8, n)), whole((PIECE, 128)), whole((1, 128))],
        out_shape=[
            jax.ShapeDtypeStruct((8, n), f32),
            jax.ShapeDtypeStruct((PIECE, 128), f32),
            jax.ShapeDtypeStruct((1, 128), f32),
        ],
        compiler_params=kernel_params(12),
        cost_estimate=work(1.2),
        name="merge",
    )(at, stats, lists)


def table_grad_kernel(
    first, many, base_ref, e_ref, *refs
):
    states, (t_ref, s_ref), out_ref = refs[:many], refs[many : many + 2], refs[-1]
    rows = out_ref.shape[0]
    per = PAD // rows
    step = first * per + pl.program_id(0)
    start = base_ref[lax.div(step, per)] + lax.rem(step, per) * rows
    ids = lax.broadcasted_iota(i32, (rows, 1), 0) + start
    total = None
    for ref, (low, high) in zip(states, spans(states)):
        part = slice(low, high)
        logits = mm_nt(e_ref[...], ref[...])
        grad = jnp.exp(logits - s_ref[0:1, part]) * s_ref[1:2, part]
        grad = jnp.where(ids == t_ref[:, part], s_ref[2:3, part], grad).astype(bf16)
        term = mm(grad, ref[...])
        total = term if total is None else total + term
    out_ref[...] = total.astype(bf16)


def table_grad(first, count, bases, table, states, targets, stats, before=None, rows=1024):
    n = NY * NZ * PIECE
    per = PAD // rows
    more = () if before is None else (before,)
    return pl.pallas_call(
        functools.partial(table_grad_kernel, first, len(states)),
        grid=(count * per,),
        in_specs=[SCALARS]
        + [pl.BlockSpec((rows, D), lambda i: (first * per + i, 0))]
        + [fixed(part.shape) for part in states]
        + [fixed((1, n)), fixed((8, n))]
        + [ANYWHERE] * len(more),
        out_specs=pl.BlockSpec((rows, D), lambda i: (first * per + i, 0)),
        out_shape=jax.ShapeDtypeStruct((NX * PAD, D), bf16),
        input_output_aliases={4 + len(states): 0} if more else {},
        compiler_params=kernel_params(32),
        cost_estimate=work(5.8 * count),
        name="table_grad",
    )(bases, table, *states, targets, stats, *more)


def embed_part_kernel(count, places, base_ref, t_ref, *refs):
    parts, out_ref = refs[:-1], refs[-1]
    rows = out_ref.shape[0]
    row = lax.broadcasted_iota(i32, (rows, 1), 0) + pl.program_id(0) * rows
    ids = jnp.where(row < count, row + base_ref[0], -1)
    total = None
    for ref, low in zip(parts, places):
        hit = (ids == t_ref[:, low : low + ref.shape[0]]).astype(bf16)
        term = mm(hit, ref[...])
        total = term if total is None else total + term
    out_ref[...] = total


def embed_part(count, base, tokens, parts, places, rows=1024):
    width = parts[0].shape[1]
    return pl.pallas_call(
        functools.partial(embed_part_kernel, count, places),
        grid=(PAD // rows,),
        in_specs=[SCALARS, fixed(tokens.shape)] + [fixed(part.shape) for part in parts],
        out_specs=pl.BlockSpec((rows, width), lambda i: (i, 0)),
        out_shape=jax.ShapeDtypeStruct((PAD, width), f32),
        compiler_params=kernel_params(28),
        cost_estimate=work(1.4 * sum(part.shape[0] for part in parts) / PAD),
        name="embed_part",
    )(base, tokens, *parts)


def embed_end_kernel(
    count, base_ref, t_ref, a_ref, b_ref, left_ref, right_ref, h_ref, m_ref, out_ref, sum_ref
):
    rows = out_ref.shape[0]
    step = pl.program_id(0)
    row = lax.broadcasted_iota(i32, (rows, 1), 0) + step * rows
    ids = jnp.where(row < count, row + base_ref[0], -1)
    left = left_ref[...]
    for ref, low in ((a_ref, 2 * PAD), (b_ref, 2 * PAD + PAD // 2)):
        hit = (ids == t_ref[:, low : low + PAD // 2]).astype(bf16)
        left = left + mm(hit, ref[...])
    total = jnp.concatenate([left, right_ref[...]], axis=1) + h_ref[...].astype(f32)
    out_ref[...] = total
    total = jnp.where(row < count, total, 0.0)
    square = jnp.sum(total * total, axis=0, keepdims=True)
    square = jnp.broadcast_to(jnp.sum(square, axis=1, keepdims=True), (8, 128))
    top = lax.broadcasted_iota(i32, (8, 128), 0) < 4

    @pl.when(step == 0)
    def _():
        sum_ref[...] = m_ref[...] + jnp.where(top, square, 0.0)

    @pl.when(step > 0)
    def _():
        sum_ref[...] += jnp.where(top, square, 0.0)


def embed_end(count, base, tokens, halves, left, right, head_part, sums, rows=256):
    return pl.pallas_call(
        functools.partial(embed_end_kernel, count),
        grid=(PAD // rows,),
        in_specs=[SCALARS, fixed(tokens.shape)]
        + [fixed(half.shape) for half in halves]
        + [pl.BlockSpec((rows, HALF), lambda i: (i, 0))] * 2
        + [pl.BlockSpec((rows, D), lambda i: (i, 0)), fixed((8, 128))],
        out_specs=[pl.BlockSpec((rows, D), lambda i: (i, 0)), whole((8, 128))],
        out_shape=[jax.ShapeDtypeStruct((PAD, D), f32), jax.ShapeDtypeStruct((8, 128), f32)],
        compiler_params=kernel_params(20),
        cost_estimate=work(3),
        name="embed_end",
    )(base, tokens, *halves, left, right, head_part, sums)


def sum_yz_kernel(q_ref, up_ref, cols_ref, out_ref):
    total = sum32([q_ref[k] for k in range(NY * NZ)])
    rows = up_ref.shape[0] // NX
    split = NX * rows
    out_ref[...] = jnp.concatenate(
        [total[split : split + rows], total[split + rows : split + 2 * rows, : D - 3 * HW]], axis=1
    )
    gains = total[split + 2 * rows : split + 2 * rows + 1]
    width = gains.shape[1] // 2
    gains = gains[:, :width] + gains[:, width:]
    per = width // NX
    for x in range(NX):
        part = slice(x * rows, (x + 1) * rows)
        lines = jnp.concatenate([total[part], up_ref[part, :]], axis=1)
        mine = gains[:, x * per : (x + 1) * per]
        high = mine.astype(bf16).astype(f32)
        last = jnp.concatenate(
            [high, mine - high, jnp.zeros((1, lines.shape[1] - 2 * per), f32)], axis=1
        )
        last = jnp.concatenate([last, jnp.zeros((7, lines.shape[1]), f32)], axis=0)
        cols_ref[x] = jnp.concatenate([lines, last], axis=0).astype(bf16)


def sum_yz(parts, up):
    rows = up.shape[0] // NX
    shapes = [((NX, rows + 8, 3 * HW + up.shape[1]), bf16), ((rows, D), f32)]
    return pl.pallas_call(
        sum_yz_kernel,
        grid=(1,),
        in_specs=[fixed(parts.shape), fixed(up.shape)],
        out_specs=[whole(s) for s, _ in shapes],
        out_shape=[jax.ShapeDtypeStruct(s, t) for s, t in shapes],
        compiler_params=kernel_params(16),
        cost_estimate=work(2),
        name="sum_yz",
    )(parts, up)


def rows_grad_kernel(c_ref, o_ref, down_ref, sums_ref, out_ref, gains_ref, square_ref):
    rows = o_ref.shape[0]
    ffx = c_ref.shape[2] - 3 * HW
    cols = [c_ref[x].astype(f32) for x in range(NX)]
    parts = [cols[x][:rows, s * HW : (s + 1) * HW] for s in range(3) for x in range(NX)]
    parts += [o_ref[...]] + [cols[x][:rows, 3 * HW : 3 * HW + ffx] for x in range(NX)]
    total = jnp.concatenate(parts, axis=1)
    out_ref[...] = total
    gains = sum(cols[x][rows : rows + 1] for x in range(NX))
    width = 3 * rows
    gains = gains[:, :width] + gains[:, width : 2 * width]
    gains_ref[...] = gains
    squares = [jnp.sum(v * v, axis=0, keepdims=True) for v in (total, down_ref[...], gains)]
    square = sum(jnp.sum(v, axis=1, keepdims=True) for v in squares)
    square_ref[...] = jnp.concatenate(
        [jnp.broadcast_to(square, (4, 128)), jnp.broadcast_to(sums_ref[...], (4, 128))], axis=0
    )


def rows_grad(cols, out, down, sums):
    rows, width = out.shape[0], NX * cols.shape[2] + D
    shapes = [(rows, width), (1, 3 * rows), (8, 128)]
    return pl.pallas_call(
        rows_grad_kernel,
        grid=(1,),
        in_specs=[fixed(v.shape) for v in (cols, out, down, sums)],
        out_specs=[whole(s) for s in shapes],
        out_shape=[jax.ShapeDtypeStruct(s, f32) for s in shapes],
        compiler_params=kernel_params(16),
        cost_estimate=work(2),
        name="rows_grad",
    )(cols, out, down, sums)


def adam(start, gradient, moment, square, step_rate):
    moment_new = BETA_ONE * moment + (1.0 - BETA_ONE) * gradient
    square_new = BETA_TWO * square + (1.0 - BETA_TWO) * gradient * gradient
    fixed_moment = moment_new / (1.0 - BETA_ONE**STEP)
    fixed_square = square_new / (1.0 - BETA_TWO**STEP)
    moved = start - step_rate * (fixed_moment / (jnp.sqrt(fixed_square) + ADAM_EPS))
    return (moved, moment_new, square_new)


def per_device(
    token_ids,
    targets,
    segments,
    domains,
    embedding,
    w_rows,
    w_down,
    norm_gains,
    first_embed,
    first_rows,
    first_down,
    first_gains,
    second_embed,
    second_rows,
    second_down,
    second_gains,
    delta_embed,
    delta_rows,
    delta_down,
    delta_gains,
    outer_embed,
    outer_rows,
    outer_down,
    outer_gains,
):
    xi, yi, zi = (lax.axis_index(axis) for axis in ("x", "y", "z"))
    at = jnp.stack([xi, yi, zi])
    mine = (xi * NY + yi) * NZ + zi
    count = embedding.shape[1]
    rows_in = w_rows.shape[1]
    shards = NX * NY * NZ
    ffx = w_down.shape[1] * shards // NX
    back = jnp.arange(4, dtype=i32)
    bases_x = ((back * NY + yi) * NZ + zi) * count
    bases_y = ((xi * NY + (yi - back) % NY) * NZ + zi) * count
    key_bases = (
        (((xi - back[None, :]) % NX) * NY + (yi - back[:, None]) % NY) * PIECE
    ).reshape(-1)

    own = jnp.pad(embedding[0].astype(bf16), ((0, PAD - count), (0, 0)))
    table = lax.all_gather(own, "x", axis=0, tiled=True)

    rows_low = w_rows[0].astype(bf16)
    down_low = w_down[0].astype(bf16)

    def by_x(start_col, width):
        block = rows_low[:, start_col : start_col + NX * width]
        return jnp.transpose(block.reshape(rows_in, NX, width), (1, 0, 2))

    def pair_z(value):
        other = shift(value, "z", 1)
        return jnp.where(zi == 0, jnp.stack([value, other]), jnp.stack([other, value]))

    def whole_rows(value):
        return jnp.transpose(value, (2, 0, 1, 3, 4)).reshape(D, -1)

    gain_cols = norm_gains.shape[2]
    info = jnp.concatenate([token_ids[0], targets[0], segments[0], domains[0]], axis=0)
    gains_low = jnp.pad(norm_gains[0].astype(bf16), ((0, 5), (0, 0)))
    info = jnp.concatenate([(info // 256).astype(bf16), (info % 256).astype(bf16), gains_low], axis=1)
    info = jnp.pad(info, ((0, 0), (0, 3 * HW - info.shape[1])))
    cols = [by_x(0, HW), by_x(D, HW), by_x(2 * D, HW), by_x(4 * D, ffx)]
    cols = jnp.concatenate(cols, axis=2)
    info = jnp.pad(info, ((0, 0), (0, ffx)))
    cols = jnp.concatenate([cols, jnp.broadcast_to(info, (NX,) + info.shape)], axis=1)
    cols = lax.all_to_all(cols, "x", 0, 0, tiled=True)
    lines = cols.shape[1]
    early = jnp.concatenate(
        [
            cols[:, :, : 3 * HW].reshape(NX * lines, 3 * HW),
            rows_low[:, 3 * D : 4 * D].reshape(-1, 3 * HW),
        ],
        axis=0,
    )
    late = jnp.concatenate(
        [cols[:, :rows_in, 3 * HW :].reshape(NX * rows_in, ffx), down_low], axis=0
    )
    early, late = pair_z(early), pair_z(late)
    early = order_y(at, gather_rel(early, "y"))
    late = gather_rel(late, "y")
    w_out = early[:, :, NX * lines :].reshape(HW, D)
    cols = early[:, :, : NX * lines].reshape(NY, NZ, NX, lines, 3 * HW)
    w_qkv = whole_rows(cols[:, :, :, :rows_in])
    info = cols[:, :, :, rows_in:, : 128 + gain_cols].astype(f32)
    gain = info[:, :, :, :3, 128:]
    gain = jnp.transpose(gain, (3, 2, 0, 1, 4)).reshape(3, D)
    frequency = jnp.exp(jnp.arange(HD // 2, dtype=f32) * (-math.log(10000.0) / (HD // 2)))
    frequency = jnp.broadcast_to(frequency[:, None], (HD // 2, 128))
    columns, lists, places, tokens_y, tokens_x, counts, cosine, sine = prep(
        at, info[..., :128].reshape(shards, lines - rows_in, 128), key_bases, frequency
    )
    counts = counts[:NDOM, 0]
    targets_row = lists[:, :PAD].astype(i32)

    found = lookup(bases_x, columns, 0, table)
    w_outs = lax.all_gather(tie(w_out, table), "x")
    wanted = lookup(tie(bases_x, found), columns, 2, table)
    parts = scatter_rel([found[k * NZ * PIECE : (k + 1) * NZ * PIECE] for k in range(NY)], "y")
    parts, wanted, late = lax.optimization_barrier((parts, wanted, late))
    late = order_y(at, late)
    split = NX * rows_in
    w_up = whole_rows(late[:, :, :split].reshape(NY, NZ, NX, rows_in, ffx))
    w_dn = late[:, :, split:].reshape(ffx, D)
    found = sum32(parts).astype(bf16)
    x0_own = sum32(scatter_rel([found[:PIECE], found[PIECE:]], "z"))
    x0_pieces = gather_rel(x0_own.astype(bf16), "x")

    x0, a, q, kv = qkv(x0_pieces, gain[0:1], w_qkv, cosine, sine)
    kvs = gather_rel(kv, "y")
    lead = delta_down.shape[1]
    delta_tail = jnp.concatenate(
        [delta_down[0], jnp.pad(delta_gains[0], ((0, 5), (0, D - gain_cols)))], axis=0
    )
    summed = lax.psum((delta_embed[0], delta_rows[0], delta_tail), ("zh", "c"))
    wanted = tie(wanted, (kvs, summed))
    wanted = lax.psum_scatter(wanted, "y", scatter_dimension=0, tiled=True)
    o, lse_q = attend(key_bases, q, kvs, places)
    os = gather_rel(o, "x")
    x1 = x0.astype(f32)
    for s, heads in enumerate(os):
        pieces = [heads[((j - s) % NX) * PIECE : ((j - s) % NX + 1) * PIECE] for j in range(NX)]
        heads = jnp.concatenate(pieces, axis=0) if s else heads
        x1 = x1 + mm(heads, lax.dynamic_index_in_dim(w_outs, (xi - s) % NX, 0, False))

    b = rms_norm(x1, gain[1]).astype(bf16)
    up = mm(b, w_up)
    hmid = jax.nn.gelu(up).astype(bf16)
    part = mm(hmid, w_dn).astype(bf16).reshape(NX, PIECE, D)
    parts = scatter_rel([part[k] for k in range(NX)], "x")
    target_rows = scatter_rel([wanted[:PIECE], wanted[PIECE:]], "z")
    parts, target_rows = lax.optimization_barrier((parts, target_rows))
    x2 = x1[:PIECE] + sum32(parts)
    hf = rms_norm(x2, gain[2]).astype(bf16)

    hf_pair = jnp.concatenate(gather_rel(hf, "z"), axis=0)
    states = gather_ring(hf_pair, "y")
    summed = tie(summed, hf_pair)
    summed = (summed[0], summed[1], summed[2][:lead], summed[2][lead : lead + 3, :gain_cols])
    group_count = lax.axis_size("zh") * lax.axis_size("c")
    weights_now = (embedding[0], w_rows[0], w_down[0], norm_gains[0])
    outers = (outer_embed, outer_rows, outer_down, outer_gains)
    means = [part_sum / group_count for part_sum in summed]
    momenta = [OUTER_MU * outer + mean for outer, mean in zip(outers, means)]
    starts = []
    for kind_index in range(4):
        shrink = 1.0 - (0.0 if kind_index == 3 else RATE * DECAY)
        starts.append(
            shrink * weights_now[kind_index]
            - OUTER_RATE * (means[kind_index] + OUTER_MU * momenta[kind_index])
        )

    states, means, momenta, starts = lax.optimization_barrier((states, means, momenta, starts))
    *rest_sum, stats = head(count, bases_x, states, table, columns)
    stats = lax.all_to_all(stats, ("y", "z"), 0, 0, tiled=True)
    terms = [rest_sum[0]]
    for index in range(1, NY * NZ):
        ky, kz = index // NZ, index % NZ
        perm = [
            (y * NZ + z, ((y - ky) % NY) * NZ + (z - kz) % NZ)
            for y in range(NY)
            for z in range(NZ)
        ]
        terms.append(lax.ppermute(rest_sum[index], ("y", "z"), perm))
    stats, scales, sums_own = merge(at, stats, lists)
    def head_grad(first, many, after, before=None):
        return table_grad(
            first, many, tie(bases_x, after), table, states, targets_row, stats, before
        )

    from_head = head_grad(0, 2, stats)
    terms, from_head = lax.optimization_barrier((terms, from_head))
    d_hf = -scales[:, NY * NZ : NY * NZ + 1] * sum32(target_rows)
    for index, term in enumerate(terms):
        d_hf = d_hf + scales[:, index : index + 1] * term.astype(f32)

    dx2, gain_two = rms_back(x2, gain[2], d_hf)
    dx2_low = dx2.astype(bf16)
    g2 = gather_rel(dx2_low, "x")
    from_head = head_grad(2, 1, dx2_low, from_head)
    g2, from_head = lax.optimization_barrier((g2, from_head))
    g2 = jnp.concatenate(g2, axis=0)
    unused, pull_gelu = jax.vjp(jax.nn.gelu, up)
    d_up = pull_gelu(mm_nt(g2, w_dn))[0].astype(bf16)
    part = mm_nt(d_up, w_up).astype(bf16)
    d_b = scatter_rel([part[k * PIECE : (k + 1) * PIECE] for k in range(NX)], "x")

    def to_yz(value):
        value = value.astype(bf16).reshape(NX, NY * NZ, rows_in, value.shape[1])
        return jnp.transpose(value, (1, 0, 2, 3)).reshape(NY * NZ, NX * rows_in, -1)

    def scatter_yz(value):
        value = lax.all_to_all(value, ("y", "z"), 0, 0, tiled=True)
        return sum32([value[k] for k in range(NY * NZ)])

    from_head = head_grad(3, 1, part, from_head)
    d_b, from_head = lax.optimization_barrier((d_b, from_head))
    d_b = sum32(d_b)

    d_norm, gain_one = rms_back(x1[:PIECE], gain[1], d_b)
    dx1 = dx2 + d_norm
    dx1_low = dx1.astype(bf16)
    g1 = gather_rel(dx1_low, "x")
    g2_low, d_up_low = tie((g2, d_up), dx1_low)
    ffn_grad = jnp.concatenate(
        [
            to_yz(mm_tn(b, d_up_low)),
            mm_tn(hmid, g2_low).astype(bf16).reshape(NY * NZ, -1, D),
        ],
        axis=1,
    )
    g1, ffn_grad = lax.optimization_barrier((g1, ffn_grad))
    from_head = lax.psum_scatter(from_head, "x", scatter_dimension=0, tiled=True)
    ffn_grad = ffn_grad.reshape(NY, NZ, -1, D)
    ffn_own = lax.dynamic_index_in_dim(ffn_grad, zi, 1, False)
    ffn_other = shift(lax.dynamic_index_in_dim(ffn_grad, 1 - zi, 1, False), "z", 1)
    dq, *dkvs = attend_back(key_bases, q, kvs, places, lse_q, g1, w_out)
    g1_low = jnp.concatenate(tie(g1, dkvs[0]), axis=0)
    out_grad = mm_tn(o, g1_low).astype(bf16)
    dkvs = scatter_rel(dkvs, "y")
    dkvs, out_grad = lax.optimization_barrier((dkvs, out_grad))
    d_mixed, part, gain_zero = qkv_back(dq, dkvs, cosine, sine, w_qkv, x0)
    d_a = scatter_rel([part[k * PIECE : (k + 1) * PIECE] for k in range(NX)], "x")
    qkv_grad = to_yz(mm_tn(a, tie(d_mixed, part)))
    gains_grad = jnp.stack([gain_zero[0], gain_one, gain_two])
    gains_grad = gains_grad.reshape(3, NX, NY * NZ, gain_cols).transpose(2, 1, 0, 3)
    gains_grad = gains_grad.reshape(NY * NZ, -1)
    high = lax.reduce_precision(gains_grad, 8, 7)
    gains_grad = jnp.concatenate([high, gains_grad - high], axis=1)
    gains_grad = jnp.pad(gains_grad[:, None, :], ((0, 0), (0, 15), (0, 0)))
    out_grad = out_grad.reshape(NY * NZ, rows_in, D)
    out_rest = jnp.pad(out_grad[:, :, 3 * HW :], ((0, 0), (0, 0), (0, 6 * HW - D)))
    qkv_grad = jnp.concatenate(
        [qkv_grad, out_grad[:, :, : 3 * HW], out_rest, gains_grad.astype(bf16)], axis=1
    )
    d_a, ffn_other, qkv_grad = lax.optimization_barrier((d_a, ffn_other, qkv_grad))
    ffn_grad = (ffn_own.astype(f32) + ffn_other.astype(f32)).astype(bf16)
    d_norm, unused = rms_back(x0_own, gain[0], sum32(d_a))
    gz = (dx1 + d_norm).astype(bf16)

    gz_pair = jnp.concatenate(gather_rel(gz, "z"), axis=0)
    qkv_grad = lax.all_to_all(tie(qkv_grad, gz_pair), ("y", "z"), 0, 0, tiled=True)
    by_x, by_y = gather_rel(gz_pair[:, HALF:], "y"), gather_rel(gz_pair[:, :HALF], "x")
    by_x, by_y = lax.optimization_barrier((by_x, by_y))
    by_x = lax.all_gather(jnp.concatenate(by_x, axis=0), "x", axis=0, tiled=True)
    ffn_grad = lax.psum_scatter(
        tie(ffn_grad, (from_head, by_y)).reshape(-1, D), "y", scatter_dimension=0, tiled=True
    )
    by_y = gather_ring(jnp.concatenate(by_y, axis=0), "y")
    base_own = (mine * count).reshape(1)

    ffn_own = ffn_grad.astype(f32)
    split = NX * rows_in
    down_own = ffn_own[split:]
    cols_grad, out_own = sum_yz(qkv_grad, ffn_own[:split])
    cols_grad = lax.all_to_all(cols_grad, "x", 0, 0, tiled=True)
    rows_own, gains_own, sums = rows_grad(cols_grad, out_own, down_own, sums_own)
    gains_own = gains_own.reshape(3, gain_cols)

    left = embed_part(
        count, base_own, tokens_y, [by_y[0], by_y[1], by_y[4]], (0, PAD, 3 * PAD)
    )
    right = embed_part(count, base_own, tokens_x, [by_x], (0,))
    halves, left, right, sums = lax.optimization_barrier((by_y[2:4], left, right, sums))
    table, totals = embed_end(
        count, base_own, tokens_y, halves, left, right, from_head, sums
    )

    gradients = (table[:count], rows_own, down_own, gains_own)
    totals = all_sum(totals)
    domain_sums = totals[4, :NDOM]
    size_now = jnp.sqrt(totals[0, 0])
    factor = jnp.minimum(1.0, CLIP / size_now)

    firsts = (first_embed[0], first_rows[0], first_down[0], first_gains[0])
    seconds = (second_embed[0], second_rows[0], second_down[0], second_gains[0])
    new_items, moment_items, square_items = ([], [], [])
    for kind_index in range(4):
        moved, moment_new, square_new = adam(
            starts[kind_index],
            gradients[kind_index] * factor,
            firsts[kind_index],
            seconds[kind_index],
            GAIN_RATE if kind_index == 3 else RATE,
        )
        new_items.append(moved[None])
        moment_items.append(moment_new[None])
        square_items.append(square_new[None])
    return (
        domain_sums[None],
        counts[None],
        size_now.reshape(1),
        *new_items,
        *moment_items,
        *square_items,
        *means,
        *momenta,
    )


def solution(mesh):
    groups = mesh.shape["group"]
    high = 2 if groups % 2 == 0 else 1
    fine = Mesh(
        mesh.devices.reshape(high, groups // high, NX, NY, NZ), ("zh", "c", "x", "y", "z")
    )
    group, blk = ("zh", "c"), ("x", "y", "z")
    tokens = P(group, None, blk)
    rows = P(group, blk, None)
    gains = P(group, None, blk)
    kind = (rows, rows, rows, gains)
    shared = (P(blk, None), P(blk, None), P(blk, None), P(None, blk))
    return jax.shard_map(
        per_device,
        mesh=fine,
        in_specs=(tokens,) * 4 + kind * 4 + shared,
        out_specs=(P(group, None), P(group, None), P(group)) + kind * 3 + shared * 2,
        check_vma=False,
    )
```

```python
import functools
import math

import jax
import jax.numpy as jnp
from jax import lax
from jax.experimental import pallas as pl
from jax.experimental.pallas import tpu as pltpu
from jax.sharding import Mesh, PartitionSpec as P

D = 768
HD = 64
NDOM = 4
STEP = 10
SEGS = 8
PAD = 1024
LEFT = D // 3

EPS = 1e-06
BETA_ONE = 0.9
BETA_TWO = 0.95
ADAM_EPS = 1e-08
DECAY = 0.1
RATE = 0.02
GAIN_RATE = 0.2
CLIP = 0.05
OUTER_RATE = 0.7
OUTER_MU = 0.9

NX, NY, NZ = 4, 4, 2
SIZE = {"x": NX, "y": NY, "z": NZ}
PIECE = 128
BLOCK = NX * PIECE
HEADS = D // HD // NX
HW = HEADS * HD
NEG = -1e30

bf16, f32, i32 = jnp.bfloat16, jnp.float32, jnp.int32


def shift(value, axis, step):
    size = SIZE[axis]
    return lax.ppermute(value, axis, [(i, (i + step) % size) for i in range(size)])


def gather_rel(value, axis):
    return [value] + [shift(value, axis, k) for k in range(1, SIZE[axis])]


def scatter_rel(parts, axis):
    return [parts[0]] + [shift(parts[k], axis, -k) for k in range(1, SIZE[axis])]


def gather_ring(value, axis):
    half = value.shape[0] // 2
    before, after = shift(value, axis, 1), shift(value, axis, -1)
    first, second = shift(before[:half], axis, 1), shift(after[half:], axis, -1)
    return [value, before, first, second, after]


def spans(parts):
    start, found = 0, []
    for part in parts:
        found.append((start, start + part.shape[0]))
        start += part.shape[0]
    return found


def sum32(parts):
    total = parts[0].astype(f32)
    for part in parts[1:]:
        total = total + part.astype(f32)
    return total


def all_sum(value):
    for axis in ("z", "y", "x"):
        value = functools.reduce(jnp.add, gather_rel(value, axis))
    return value


def mm(a, b):
    return jnp.dot(a, b, preferred_element_type=f32)


def mm_nt(a, b):
    return lax.dot_general(a, b, (((1,), (1,)), ((), ())), preferred_element_type=f32)


def mm_tn(a, b):
    return lax.dot_general(a, b, (((0,), (0,)), ((), ())), preferred_element_type=f32)


def rms_norm(values, scales):
    return values * lax.rsqrt(jnp.mean(values * values, axis=-1, keepdims=True) + EPS) * scales


def rms_back(values, scales, grad):
    inverse = lax.rsqrt(jnp.mean(values * values, axis=-1, keepdims=True) + EPS)
    unit = values * inverse
    scaled = grad * scales
    grad_values = inverse * (scaled - unit * jnp.mean(scaled * unit, axis=-1, keepdims=True))
    return grad_values, jnp.sum(grad * unit, axis=0)


def tie(values, after):
    return lax.optimization_barrier((values, after))[0]


def turn_lanes(values):
    half = HD // 2
    parts = []
    for start in range(0, values.shape[1], HD):
        parts += [values[:, start + half : start + HD], values[:, start : start + half]]
    return jnp.concatenate(parts, axis=1)


def whole(shape):
    return pl.BlockSpec(shape, lambda *_: (0,) * len(shape))


def fixed(shape):
    return pl.BlockSpec(shape, lambda *_: (0,) * len(shape), pipeline_mode=pl.Buffered(1))


def kernel_params(mib):
    return pltpu.CompilerParams(vmem_limit_bytes=mib * 2**20)


def work(micros):
    return pl.CostEstimate(
        flops=int(micros * 1e9), bytes_accessed=int(micros * 3e6), transcendentals=0
    )


SCALARS = pl.BlockSpec(memory_space=pltpu.SMEM)
ANYWHERE = pl.BlockSpec(memory_space=pl.ANY)


def prep_kernel(
    at_ref, info_ref, base_ref, freq_ref, cols_ref, lists_ref, rows_ref, by_y_ref, by_x_ref, misc_ref, cos_ref, sin_ref
):
    xi, yi, first = at_ref[0], at_ref[1], at_ref[2] == 0

    def tile(y, x):
        halves = []
        for z in range(NZ):
            block = info_ref[(y * NZ + z) * NX + x]
            halves.append(block[:, :64] * 256.0 + block[:, 64:128])
        return jnp.concatenate(halves, axis=1)

    def row(block, kind, other):
        low, high = block[2 * kind : 2 * kind + 1], block[2 * kind + 1 : 2 * kind + 2]
        return jnp.where(first, high, low) if other else jnp.where(first, low, high)

    def lanes(parts):
        return jnp.concatenate(parts, axis=1)

    def pairs(blocks, kind):
        return [row(block, kind, zr) for block in blocks for zr in range(NZ)]

    near = [
        [tile(lax.rem(yi + NY - yb, NY), lax.rem(xi + NX - xb, NX)) for xb in range(NX)]
        for yb in range(NY)
    ]
    flat = [block for line in near for block in line]
    over_y, over_x = [line[0] for line in near], near[0]
    counts = []
    for d in range(NDOM):
        hits = sum(jnp.where(r == float(d), 1.0, 0.0) for r in pairs(flat, 3))
        counts.append(jnp.sum(hits, axis=1, keepdims=True))
    domain = lanes(pairs(over_y, 3))
    weight = jnp.zeros_like(domain)
    for d in range(NDOM):
        weight = jnp.where(domain == float(d), 1.0 / (NDOM * counts[d]), weight)
    lists_ref[...] = lanes(pairs(over_y, 1) + [domain, weight])
    along_y = [tile(y, xi) for y in range(NY)]
    columns = zip(
        pairs(over_y, 0), pairs(over_y, 1), pairs(along_y, 1)
    )
    for k, parts in enumerate(columns):
        square = jnp.concatenate(
            list(parts) + [jnp.zeros((PIECE - len(parts), PIECE), f32)], axis=0
        )
        cols_ref[k * PIECE : (k + 1) * PIECE, :] = jnp.transpose(square).astype(i32)
    seg, seg_own = lanes([row(b, 2, 0) for b in flat]), lanes([row(b, 2, 0) for b in over_x])
    lane = lax.broadcasted_iota(i32, (1, PIECE), 1)
    place = lanes([lane + base_ref[xb] for xb in range(NX)])
    start = jnp.zeros((1, BLOCK), i32)
    for s in range(1, SEGS):
        before = jnp.sum(jnp.where(seg < float(s), 1.0, 0.0), axis=1, keepdims=True)
        start = jnp.where(seg_own == float(s), before.astype(i32), start)
    rows_ref[...] = jnp.concatenate(
        [place, place - start, jnp.zeros((6, BLOCK), i32)], axis=0
    )
    by_x = []
    for x in range(NX):
        blocks = [tile(lax.rem(yi + NY - yb, NY), x) for yb in range(NY)]
        by_x += [row(block, 0, zr) for zr in range(NZ) for block in blocks]
    by_y_ref[...] = lanes(pairs(flat, 0)).astype(i32)
    by_x_ref[...] = lanes(by_x).astype(i32)
    misc_ref[...] = jnp.concatenate(
        [jnp.broadcast_to(c, (1, 128)) for c in counts] + [jnp.zeros((4, 128), f32)], axis=0
    )
    angle = (place - start).astype(f32) * freq_ref[:, :1]
    cosine, sine = jnp.cos(angle), jnp.sin(angle)
    cos_ref[...] = jnp.transpose(jnp.concatenate([cosine] * 4, axis=0))
    sin_ref[...] = jnp.transpose(jnp.concatenate([-sine, sine] * 2, axis=0))


def prep(at, info, bases, frequency):
    shapes = [
        ((PAD, 128), i32),
        ((1, 3 * PAD), f32),
        ((8, BLOCK), i32),
        ((1, 4 * PAD), i32),
        ((1, 4 * PAD), i32),
        ((8, 128), f32),
        ((BLOCK, 128), f32),
        ((BLOCK, 128), f32),
    ]
    return pl.pallas_call(
        prep_kernel,
        in_specs=[SCALARS, fixed(info.shape), SCALARS, fixed(frequency.shape)],
        out_specs=[whole(s) for s, _ in shapes],
        out_shape=[jax.ShapeDtypeStruct(s, t) for s, t in shapes],
        grid=(1,),
        compiler_params=kernel_params(12),
        cost_estimate=work(1.4),
        name="prep",
    )(at, info, bases, frequency)


def order_kernel(at_ref, a_ref, b_ref, c_ref, d_ref, out_ref, sem):
    copies = [
        pltpu.make_async_copy(ref, out_ref.at[lax.rem(at_ref[1] + NY - k, NY)], sem.at[k])
        for k, ref in enumerate((a_ref, b_ref, c_ref, d_ref))
    ]
    for copy in copies:
        copy.start()
    for copy in copies:
        copy.wait()


def order_y(at, parts):
    return pl.pallas_call(
        order_kernel,
        in_specs=[SCALARS] + [ANYWHERE] * NY,
        out_specs=ANYWHERE,
        out_shape=jax.ShapeDtypeStruct((NY,) + parts[0].shape, parts[0].dtype),
        scratch_shapes=[pltpu.SemaphoreType.DMA((NY,))],
        compiler_params=kernel_params(4),
        cost_estimate=work(2),
        name="order_y",
    )(at, *parts)


def lookup_kernel(column, base_ref, t_ref, table_ref, out_ref):
    tokens = t_ref[:, column : column + 1]
    total = None
    for k in range(NX):
        ids = lax.broadcasted_iota(i32, (1, PAD), 1) + base_ref[k]
        hit = (tokens == ids).astype(bf16)
        term = mm(hit, table_ref[k * PAD : (k + 1) * PAD, :])
        total = term if total is None else total + term
    out_ref[...] = total.astype(bf16)


def lookup(bases, tokens, column, table, rows=1024):
    n = tokens.shape[0]
    return pl.pallas_call(
        functools.partial(lookup_kernel, column),
        grid=(n // rows,),
        in_specs=[
            SCALARS,
            pl.BlockSpec((rows, 128), lambda i: (i, 0)),
            fixed(table.shape),
        ],
        out_specs=pl.BlockSpec((rows, D), lambda i: (i, 0)),
        out_shape=jax.ShapeDtypeStruct((n, D), bf16),
        compiler_params=kernel_params(28),
        cost_estimate=work(10),
        name="lookup",
    )(bases, tokens, table)


def qkv_kernel(
    a_ref, b_ref, c_ref, d_ref, g_ref, w_ref, cos_ref, sin_ref, x_ref, n_ref, q_ref, kv_ref
):
    for k, ref in enumerate((a_ref, b_ref, c_ref, d_ref)):
        rows = slice(k * PIECE, (k + 1) * PIECE)
        x_ref[rows, :] = ref[...]
        normed = rms_norm(ref[...].astype(f32), g_ref[...]).astype(bf16)
        n_ref[rows, :] = normed
        mixed = mm(normed, w_ref[...])
        turned = mixed[:, : 2 * HW]
        cosine = jnp.concatenate([cos_ref[rows, :]] * 3, axis=1)
        sine = jnp.concatenate([sin_ref[rows, :]] * 3, axis=1)
        turned = turned * cosine + turn_lanes(turned) * sine
        q_ref[rows, :] = turned[:, :HW].astype(bf16)
        kv_ref[rows, :] = jnp.concatenate([turned[:, HW:], mixed[:, 2 * HW :]], axis=1).astype(
            bf16
        )


def qkv(pieces, gain, weights, cosine, sine):
    shapes = [(BLOCK, D), (BLOCK, D), (BLOCK, HW), (BLOCK, 2 * HW)]
    return pl.pallas_call(
        qkv_kernel,
        grid=(1,),
        in_specs=[fixed((PIECE, D))] * 4
        + [fixed((1, D)), fixed(weights.shape), fixed(cosine.shape), fixed(sine.shape)],
        out_specs=[whole(s) for s in shapes],
        out_shape=[jax.ShapeDtypeStruct(s, bf16) for s in shapes],
        compiler_params=kernel_params(16),
        cost_estimate=work(2.3),
        name="qkv",
    )(*pieces, gain, weights, cosine, sine)


def qkv_back_kernel(
    dq_ref, a_ref, b_ref, c_ref, d_ref, cos_ref, sin_ref, w_ref, x_ref, mixed_ref, part_ref, gain_ref
):
    gain = None
    for k in range(NX):
        rows = slice(k * PIECE, (k + 1) * PIECE)
        dkv = sum32([ref[rows, :] for ref in (a_ref, b_ref, c_ref, d_ref)])
        turned = jnp.concatenate([dq_ref[rows, :], dkv[:, :HW]], axis=1)
        cosine = jnp.concatenate([cos_ref[rows, :]] * 3, axis=1)
        sine = jnp.concatenate([sin_ref[rows, :]] * 3, axis=1)
        raw = turned * cosine + turn_lanes(turned * sine)
        mixed = jnp.concatenate([raw, dkv[:, HW:]], axis=1).astype(bf16)
        mixed_ref[rows, :] = mixed
        part = mm_nt(mixed, w_ref[...])
        part_ref[rows, :] = part.astype(bf16)
        x = x_ref[rows, :].astype(f32)
        unit = x * lax.rsqrt(jnp.mean(x * x, axis=-1, keepdims=True) + EPS)
        share = jnp.sum(part * unit, axis=0, keepdims=True)
        gain = share if gain is None else gain + share
    gain_ref[...] = gain


def qkv_back(dq, dkvs, cosine, sine, weights, x0):
    shapes = [((BLOCK, 3 * HW), bf16), ((BLOCK, D), bf16), ((1, D), f32)]
    return pl.pallas_call(
        qkv_back_kernel,
        grid=(1,),
        in_specs=[fixed((BLOCK, HW))]
        + [fixed((BLOCK, 2 * HW))] * 4
        + [fixed(cosine.shape), fixed(sine.shape), fixed(weights.shape), fixed(x0.shape)],
        out_specs=[whole(s) for s, _ in shapes],
        out_shape=[jax.ShapeDtypeStruct(s, t) for s, t in shapes],
        compiler_params=kernel_params(16),
        cost_estimate=work(2),
        name="qkv_back",
    )(dq, *dkvs, cosine, sine, weights, x0)


def fill_bias(base_ref, rows_ref, bias_ref):
    query, reach = rows_ref[0:1, :], rows_ref[1:2, :]
    key = lax.broadcasted_iota(i32, (PIECE, BLOCK), 0)
    for j in range(NX * NY):
        back = (query - base_ref[j]) - key
        bias_ref[j * PIECE : (j + 1) * PIECE, :] = jnp.where(
            (back >= 0) & (back <= reach), 0.0, NEG
        )


def attend_kernel(
    base_ref, q_ref, a_ref, b_ref, c_ref, d_ref, rows_ref, o_ref, lse_ref, kv_ref, bias_ref
):
    pieces = (a_ref, b_ref, c_ref, d_ref)
    for ref, (low, high) in zip(pieces, spans(pieces)):
        kv_ref[low:high, :] = ref[...]
    fill_bias(base_ref, rows_ref, bias_ref)
    q = q_ref[...] * jnp.asarray(HD**-0.5, bf16)
    outs, tops = [], []
    for h in range(HEADS):
        a, b = h * HD, (h + 1) * HD
        scores = mm_nt(kv_ref[:, a:b], q[:, a:b]) + bias_ref[...]
        top = jnp.max(scores, axis=0, keepdims=True)
        weight = jnp.exp(scores - top)
        total = jnp.sum(weight, axis=0, keepdims=True)
        probs = (weight * (1.0 / total)).astype(bf16)
        outs.append(mm_tn(kv_ref[:, HW + a : HW + b], probs))
        tops.append(top + jnp.log(total))
    o_ref[...] = jnp.transpose(jnp.concatenate(outs, axis=0)).astype(bf16)
    lse_ref[...] = jnp.concatenate(tops + [jnp.zeros((8 - HEADS, BLOCK), f32)], axis=0)


def attend(bases, q, kvs, rows):
    keys = NY * BLOCK
    return pl.pallas_call(
        attend_kernel,
        grid=(1,),
        in_specs=[SCALARS, fixed((BLOCK, HW))]
        + [fixed(kv.shape) for kv in kvs]
        + [fixed((8, BLOCK))],
        out_specs=[whole((BLOCK, HW)), whole((8, BLOCK))],
        out_shape=[
            jax.ShapeDtypeStruct((BLOCK, HW), bf16),
            jax.ShapeDtypeStruct((8, BLOCK), f32),
        ],
        scratch_shapes=[pltpu.VMEM((keys, 2 * HW), bf16), pltpu.VMEM((keys, BLOCK), f32)],
        compiler_params=kernel_params(24),
        cost_estimate=work(8.5),
        name="attend",
    )(bases, q, *kvs, rows)


def attend_back_kernel(
    base_ref,
    q_ref,
    a_ref,
    b_ref,
    c_ref,
    d_ref,
    rows_ref,
    lse_ref,
    ga_ref,
    gb_ref,
    gc_ref,
    gd_ref,
    w_ref,
    dq_ref,
    da_ref,
    db_ref,
    dc_ref,
    dd_ref,
    kv_ref,
    bias_ref,
):
    pieces = (a_ref, b_ref, c_ref, d_ref)
    for ref, (low, high) in zip(pieces, spans(pieces)):
        kv_ref[low:high, :] = ref[...]
    fill_bias(base_ref, rows_ref, bias_ref)
    q = q_ref[...]
    grad = jnp.concatenate(
        [mm_nt(ref[...], w_ref[...]).astype(bf16) for ref in (ga_ref, gb_ref, gc_ref, gd_ref)],
        axis=0,
    )
    scaled = q * jnp.asarray(HD**-0.5, bf16)
    dqs, dks, dvs = [], [], []
    for h in range(HEADS):
        a, b = h * HD, (h + 1) * HD
        key = kv_ref[:, a:b]
        scores = mm_nt(key, scaled[:, a:b]) + bias_ref[...]
        probs = jnp.exp(scores - lse_ref[h : h + 1, :])
        dprobs = mm_nt(kv_ref[:, HW + a : HW + b], grad[:, a:b])
        both = probs * dprobs
        row = jnp.sum(both, axis=0, keepdims=True)
        dscores = ((both - probs * row) * HD**-0.5).astype(bf16)
        dqs.append(mm_tn(key, dscores))
        dks.append(mm(dscores, q[:, a:b]).astype(bf16))
        dvs.append(mm(probs.astype(bf16), grad[:, a:b]).astype(bf16))
    dq_ref[...] = jnp.transpose(jnp.concatenate(dqs, axis=0))
    for k, ref in enumerate((da_ref, db_ref, dc_ref, dd_ref)):
        rows = slice(k * BLOCK, (k + 1) * BLOCK)
        ref[...] = jnp.concatenate([part[rows] for part in dks + dvs], axis=1)


def attend_back(bases, q, kvs, rows, lse, grads, weights):
    keys = NY * BLOCK
    return pl.pallas_call(
        attend_back_kernel,
        grid=(1,),
        in_specs=[SCALARS, fixed((BLOCK, HW))]
        + [fixed(kv.shape) for kv in kvs]
        + [fixed((8, BLOCK)), fixed((8, BLOCK))]
        + [fixed((PIECE, D))] * 4
        + [fixed((HW, D))],
        out_specs=[whole((BLOCK, HW))] + [whole((BLOCK, 2 * HW))] * 4,
        out_shape=[jax.ShapeDtypeStruct((BLOCK, HW), f32)]
        + [jax.ShapeDtypeStruct((BLOCK, 2 * HW), bf16)] * 4,
        scratch_shapes=[pltpu.VMEM((keys, 2 * HW), bf16), pltpu.VMEM((keys, BLOCK), f32)],
        compiler_params=kernel_params(32),
        cost_estimate=work(13.5),
        name="attend_back",
    )(bases, q, *kvs, rows, lse, *grads, weights)


def head_kernel(count, many, base_ref, *refs):
    states, t_ref, far_ref = refs[:many], refs[many], refs[many + 1]
    outs = refs[many + 2 : many + 2 + NY * NZ]
    stats_ref, h_ref, table, sem = refs[many + 2 + NY * NZ :]
    copy = pltpu.make_async_copy(far_ref, table, sem)
    copy.start()
    for ref, (low, high) in zip(states, spans(states)):
        h_ref[low:high, :] = ref[...]
    copy.wait()
    targets = t_ref[:, 1:2]
    states = h_ref[...]
    column = lax.broadcasted_iota(i32, (1, PAD), 1)
    top = None
    for k in range(NX):
        block = table[k * PAD : (k + 1) * PAD, :]
        logits = mm_nt(states, block)
        cut = count // 128 * 128
        spare = jnp.where(column[:, cut:] < count, 0.0, NEG)
        logits = jnp.concatenate([logits[:, :cut], logits[:, cut:] + spare], axis=1)
        hit = targets == jnp.where(column < count, column + base_ref[k], -1)
        here = jnp.max(logits, axis=1, keepdims=True)
        found = jnp.max(jnp.where(hit, logits, NEG), axis=1, keepdims=True)
        if top is None:
            top, pick = here, found
            weight = jnp.where(hit, 0.0, jnp.exp(logits - top))
            rest = jnp.sum(weight, axis=1, keepdims=True)
            total = mm(weight.astype(bf16), block)
        else:
            higher = jnp.maximum(top, here)
            scale = jnp.exp(top - higher)
            pick = jnp.maximum(pick, found)
            weight = jnp.where(hit, 0.0, jnp.exp(logits - higher))
            rest = rest * scale + jnp.sum(weight, axis=1, keepdims=True)
            total = total * scale + mm(weight.astype(bf16), block)
            top = higher
    for k, out_ref in enumerate(outs):
        out_ref[...] = total[k * PIECE : (k + 1) * PIECE].astype(bf16)
    stats = jnp.concatenate([top, rest, pick, jnp.zeros((top.shape[0], 125), f32)], axis=1)
    stats = jnp.transpose(stats)[:8, :]
    for k in range(NY * NZ):
        stats_ref[k] = stats


def head(count, bases, states, table, targets):
    n = NY * NZ * PIECE
    return pl.pallas_call(
        functools.partial(head_kernel, count, len(states)),
        grid=(1,),
        in_specs=[SCALARS]
        + [fixed(part.shape) for part in states]
        + [fixed((n, 128)), ANYWHERE],
        out_specs=[whole((PIECE, D))] * (NY * NZ) + [whole((NY * NZ, 8, n))],
        out_shape=[jax.ShapeDtypeStruct((PIECE, D), bf16)] * (NY * NZ)
        + [jax.ShapeDtypeStruct((NY * NZ, 8, n), f32)],
        scratch_shapes=[
            pltpu.VMEM((n, D), bf16),
            pltpu.VMEM((NX * PAD, D), bf16),
            pltpu.SemaphoreType.DMA,
        ],
        compiler_params=kernel_params(38),
        cost_estimate=work(20),
        name="head",
    )(bases, *states, targets, table)


def merge_kernel(at_ref, stats_ref, lists_ref, rows_ref, cols_ref, sums_ref):
    n = NY * NZ * PIECE

    def ordered(values, k, kz):
        parts = []
        for l in range(NY):
            for zr in range(NZ):
                at = (((l - k) % NY) * NZ + (zr - kz) % NZ) * PIECE
                parts.append(values[:, at : at + PIECE])
        return jnp.concatenate(parts, axis=1)

    shards = {}
    for k in range(NY):
        for kz in range(NZ):
            y, z = lax.rem(at_ref[1] + NY - k, NY), lax.rem(at_ref[2] + NZ - kz, NZ)
            shards[k, kz] = stats_ref[y * NZ + z]
    shards = {key: ordered(values, *key) for key, values in shards.items()}
    domain, weight = lists_ref[:, n : 2 * n], lists_ref[:, 2 * n : 3 * n]
    top = functools.reduce(jnp.maximum, [s[0:1] for s in shards.values()])
    rest = sum(s[1:2] * jnp.exp(s[0:1] - top) for s in shards.values())
    pick = functools.reduce(jnp.maximum, [s[2:3] for s in shards.values()])
    total = rest + jnp.exp(pick - top)
    lse = top + jnp.log(total)
    missing = weight * (rest / total)
    rows_ref[...] = jnp.concatenate([lse, weight, -missing, jnp.zeros((5, n), f32)], axis=0)
    mine = slice(0, PIECE)
    scales = []
    for ky in range(NY):
        for kz in range(NZ):
            stats = shards[(-ky) % NY, kz]
            scales.append(weight[:, mine] * jnp.exp(stats[0:1, mine] - lse[:, mine]))
    scales += [missing[:, mine], jnp.zeros((128 - len(scales) - 1, PIECE), f32)]
    cols_ref[...] = jnp.transpose(jnp.concatenate(scales, axis=0))
    loss = lse[:, mine] - pick[:, mine]
    lane = lax.broadcasted_iota(i32, (1, 128), 1)
    sums = jnp.zeros((1, 128), f32)
    for d in range(NDOM):
        part = jnp.sum(jnp.where(domain[:, mine] == float(d), loss, 0.0), axis=1, keepdims=True)
        sums = jnp.where(lane == d, part, sums)
    sums_ref[...] = sums


def merge(at, stats, lists):
    n = NY * NZ * PIECE
    return pl.pallas_call(
        merge_kernel,
        grid=(1,),
        in_specs=[SCALARS, fixed(stats.shape), fixed(lists.shape)],
        out_specs=[whole((8, n)), whole((PIECE, 128)), whole((1, 128))],
        out_shape=[
            jax.ShapeDtypeStruct((8, n), f32),
            jax.ShapeDtypeStruct((PIECE, 128), f32),
            jax.ShapeDtypeStruct((1, 128), f32),
        ],
        compiler_params=kernel_params(12),
        cost_estimate=work(1.2),
        name="merge",
    )(at, stats, lists)


def table_grad_kernel(
    first, many, base_ref, e_ref, *refs
):
    states, (t_ref, s_ref), out_ref = refs[:many], refs[many : many + 2], refs[-1]
    rows = out_ref.shape[0]
    per = PAD // rows
    step = first * per + pl.program_id(0)
    start = base_ref[lax.div(step, per)] + lax.rem(step, per) * rows
    ids = lax.broadcasted_iota(i32, (rows, 1), 0) + start
    total = None
    for ref, (low, high) in zip(states, spans(states)):
        part = slice(low, high)
        logits = mm_nt(e_ref[...], ref[...])
        grad = jnp.exp(logits - s_ref[0:1, part]) * s_ref[1:2, part]
        grad = jnp.where(ids == t_ref[:, part], s_ref[2:3, part], grad).astype(bf16)
        term = mm(grad, ref[...])
        total = term if total is None else total + term
    out_ref[...] = total.astype(bf16)


def table_grad(first, count, bases, table, states, targets, stats, before=None, rows=1024):
    n = NY * NZ * PIECE
    per = PAD // rows
    more = () if before is None else (before,)
    return pl.pallas_call(
        functools.partial(table_grad_kernel, first, len(states)),
        grid=(count * per,),
        in_specs=[SCALARS]
        + [pl.BlockSpec((rows, D), lambda i: (first * per + i, 0))]
        + [fixed(part.shape) for part in states]
        + [fixed((1, n)), fixed((8, n))]
        + [ANYWHERE] * len(more),
        out_specs=pl.BlockSpec((rows, D), lambda i: (first * per + i, 0)),
        out_shape=jax.ShapeDtypeStruct((NX * PAD, D), bf16),
        input_output_aliases={4 + len(states): 0} if more else {},
        compiler_params=kernel_params(32),
        cost_estimate=work(5.8 * count),
        name="table_grad",
    )(bases, table, *states, targets, stats, *more)


def embed_part_kernel(count, places, base_ref, t_ref, *refs):
    parts, out_ref = refs[:-1], refs[-1]
    rows = out_ref.shape[0]
    row = lax.broadcasted_iota(i32, (rows, 1), 0) + pl.program_id(0) * rows
    ids = jnp.where(row < count, row + base_ref[0], -1)
    total = None
    for ref, low in zip(parts, places):
        hit = (ids == t_ref[:, low : low + ref.shape[0]]).astype(bf16)
        term = mm(hit, ref[...])
        total = term if total is None else total + term
    out_ref[...] = total


def embed_part(count, base, tokens, parts, places, rows=1024):
    width = parts[0].shape[1]
    return pl.pallas_call(
        functools.partial(embed_part_kernel, count, places),
        grid=(PAD // rows,),
        in_specs=[SCALARS, fixed(tokens.shape)] + [fixed(part.shape) for part in parts],
        out_specs=pl.BlockSpec((rows, width), lambda i: (i, 0)),
        out_shape=jax.ShapeDtypeStruct((PAD, width), f32),
        compiler_params=kernel_params(28),
        cost_estimate=work(1.4 * sum(part.shape[0] for part in parts) / PAD),
        name="embed_part",
    )(base, tokens, *parts)


def embed_end_kernel(
    count, base_ref, t_ref, a_ref, b_ref, left_ref, right_ref, h_ref, m_ref, out_ref, sum_ref
):
    rows = out_ref.shape[0]
    step = pl.program_id(0)
    row = lax.broadcasted_iota(i32, (rows, 1), 0) + step * rows
    ids = jnp.where(row < count, row + base_ref[0], -1)
    left = left_ref[...]
    for ref, low in ((a_ref, 2 * PAD), (b_ref, 2 * PAD + PAD // 2)):
        hit = (ids == t_ref[:, low : low + PAD // 2]).astype(bf16)
        left = left + mm(hit, ref[...])
    total = jnp.concatenate([left, right_ref[...]], axis=1) + h_ref[...].astype(f32)
    out_ref[...] = total
    total = jnp.where(row < count, total, 0.0)
    square = jnp.sum(total * total, axis=0, keepdims=True)
    square = jnp.broadcast_to(jnp.sum(square, axis=1, keepdims=True), (8, 128))
    top = lax.broadcasted_iota(i32, (8, 128), 0) < 4

    @pl.when(step == 0)
    def _():
        sum_ref[...] = m_ref[...] + jnp.where(top, square, 0.0)

    @pl.when(step > 0)
    def _():
        sum_ref[...] += jnp.where(top, square, 0.0)


def embed_end(count, base, tokens, halves, left, right, head_part, sums, rows=256):
    return pl.pallas_call(
        functools.partial(embed_end_kernel, count),
        grid=(PAD // rows,),
        in_specs=[SCALARS, fixed(tokens.shape)]
        + [fixed(half.shape) for half in halves]
        + [pl.BlockSpec((rows, LEFT), lambda i: (i, 0))]
        + [pl.BlockSpec((rows, D - LEFT), lambda i: (i, 0))]
        + [pl.BlockSpec((rows, D), lambda i: (i, 0)), fixed((8, 128))],
        out_specs=[pl.BlockSpec((rows, D), lambda i: (i, 0)), whole((8, 128))],
        out_shape=[jax.ShapeDtypeStruct((PAD, D), f32), jax.ShapeDtypeStruct((8, 128), f32)],
        compiler_params=kernel_params(20),
        cost_estimate=work(3),
        name="embed_end",
    )(base, tokens, *halves, left, right, head_part, sums)


def sum_yz_kernel(q_ref, up_ref, cols_ref, out_ref):
    total = sum32([q_ref[k] for k in range(NY * NZ)])
    rows = up_ref.shape[0] // NX
    split = NX * rows
    out_ref[...] = jnp.concatenate(
        [total[split : split + rows], total[split + rows : split + 2 * rows, : D - 3 * HW]], axis=1
    )
    gains = total[split + 2 * rows : split + 2 * rows + 1]
    width = gains.shape[1] // 2
    gains = gains[:, :width] + gains[:, width:]
    per = width // NX
    for x in range(NX):
        part = slice(x * rows, (x + 1) * rows)
        lines = jnp.concatenate([total[part], up_ref[part, :]], axis=1)
        mine = gains[:, x * per : (x + 1) * per]
        high = mine.astype(bf16).astype(f32)
        last = jnp.concatenate(
            [high, mine - high, jnp.zeros((1, lines.shape[1] - 2 * per), f32)], axis=1
        )
        last = jnp.concatenate([last, jnp.zeros((7, lines.shape[1]), f32)], axis=0)
        cols_ref[x] = jnp.concatenate([lines, last], axis=0).astype(bf16)


def sum_yz(parts, up):
    rows = up.shape[0] // NX
    shapes = [((NX, rows + 8, 3 * HW + up.shape[1]), bf16), ((rows, D), f32)]
    return pl.pallas_call(
        sum_yz_kernel,
        grid=(1,),
        in_specs=[fixed(parts.shape), fixed(up.shape)],
        out_specs=[whole(s) for s, _ in shapes],
        out_shape=[jax.ShapeDtypeStruct(s, t) for s, t in shapes],
        compiler_params=kernel_params(16),
        cost_estimate=work(2),
        name="sum_yz",
    )(parts, up)


def rows_grad_kernel(c_ref, o_ref, down_ref, sums_ref, out_ref, gains_ref, square_ref):
    rows = o_ref.shape[0]
    ffx = c_ref.shape[2] - 3 * HW
    cols = [c_ref[x].astype(f32) for x in range(NX)]
    parts = [cols[x][:rows, s * HW : (s + 1) * HW] for s in range(3) for x in range(NX)]
    parts += [o_ref[...]] + [cols[x][:rows, 3 * HW : 3 * HW + ffx] for x in range(NX)]
    total = jnp.concatenate(parts, axis=1)
    out_ref[...] = total
    gains = sum(cols[x][rows : rows + 1] for x in range(NX))
    width = 3 * rows
    gains = gains[:, :width] + gains[:, width : 2 * width]
    gains_ref[...] = gains
    squares = [jnp.sum(v * v, axis=0, keepdims=True) for v in (total, down_ref[...], gains)]
    square = sum(jnp.sum(v, axis=1, keepdims=True) for v in squares)
    square_ref[...] = jnp.concatenate(
        [jnp.broadcast_to(square, (4, 128)), jnp.broadcast_to(sums_ref[...], (4, 128))], axis=0
    )


def rows_grad(cols, out, down, sums):
    rows, width = out.shape[0], NX * cols.shape[2] + D
    shapes = [(rows, width), (1, 3 * rows), (8, 128)]
    return pl.pallas_call(
        rows_grad_kernel,
        grid=(1,),
        in_specs=[fixed(v.shape) for v in (cols, out, down, sums)],
        out_specs=[whole(s) for s in shapes],
        out_shape=[jax.ShapeDtypeStruct(s, f32) for s in shapes],
        compiler_params=kernel_params(16),
        cost_estimate=work(2),
        name="rows_grad",
    )(cols, out, down, sums)


def adam(start, gradient, moment, square, step_rate):
    moment_new = BETA_ONE * moment + (1.0 - BETA_ONE) * gradient
    square_new = BETA_TWO * square + (1.0 - BETA_TWO) * gradient * gradient
    fixed_moment = moment_new / (1.0 - BETA_ONE**STEP)
    fixed_square = square_new / (1.0 - BETA_TWO**STEP)
    moved = start - step_rate * (fixed_moment / (jnp.sqrt(fixed_square) + ADAM_EPS))
    return (moved, moment_new, square_new)


def per_device(
    token_ids,
    targets,
    segments,
    domains,
    embedding,
    w_rows,
    w_down,
    norm_gains,
    first_embed,
    first_rows,
    first_down,
    first_gains,
    second_embed,
    second_rows,
    second_down,
    second_gains,
    delta_embed,
    delta_rows,
    delta_down,
    delta_gains,
    outer_embed,
    outer_rows,
    outer_down,
    outer_gains,
):
    xi, yi, zi = (lax.axis_index(axis) for axis in ("x", "y", "z"))
    at = jnp.stack([xi, yi, zi])
    mine = (xi * NY + yi) * NZ + zi
    count = embedding.shape[1]
    rows_in = w_rows.shape[1]
    shards = NX * NY * NZ
    ffx = w_down.shape[1] * shards // NX
    back = jnp.arange(4, dtype=i32)
    bases_x = ((back * NY + yi) * NZ + zi) * count
    bases_y = ((xi * NY + (yi - back) % NY) * NZ + zi) * count
    key_bases = (
        (((xi - back[None, :]) % NX) * NY + (yi - back[:, None]) % NY) * PIECE
    ).reshape(-1)

    own = jnp.pad(embedding[0].astype(bf16), ((0, PAD - count), (0, 0)))
    table = lax.all_gather(own, "x", axis=0, tiled=True)

    rows_low = w_rows[0].astype(bf16)
    down_low = w_down[0].astype(bf16)

    def by_x(start_col, width):
        block = rows_low[:, start_col : start_col + NX * width]
        return jnp.transpose(block.reshape(rows_in, NX, width), (1, 0, 2))

    def pair_z(value):
        other = shift(value, "z", 1)
        return jnp.where(zi == 0, jnp.stack([value, other]), jnp.stack([other, value]))

    def whole_rows(value):
        return jnp.transpose(value, (2, 0, 1, 3, 4)).reshape(D, -1)

    gain_cols = norm_gains.shape[2]
    info = jnp.concatenate([token_ids[0], targets[0], segments[0], domains[0]], axis=0)
    gains_low = jnp.pad(norm_gains[0].astype(bf16), ((0, 5), (0, 0)))
    info = jnp.concatenate([(info // 256).astype(bf16), (info % 256).astype(bf16), gains_low], axis=1)
    info = jnp.pad(info, ((0, 0), (0, 3 * HW - info.shape[1])))
    cols = [by_x(0, HW), by_x(D, HW), by_x(2 * D, HW), by_x(4 * D, ffx)]
    cols = jnp.concatenate(cols, axis=2)
    info = jnp.pad(info, ((0, 0), (0, ffx)))
    cols = jnp.concatenate([cols, jnp.broadcast_to(info, (NX,) + info.shape)], axis=1)
    cols = lax.all_to_all(cols, "x", 0, 0, tiled=True)
    lines = cols.shape[1]
    early = jnp.concatenate(
        [
            cols[:, :, : 3 * HW].reshape(NX * lines, 3 * HW),
            rows_low[:, 3 * D : 4 * D].reshape(-1, 3 * HW),
        ],
        axis=0,
    )
    late = jnp.concatenate(
        [cols[:, :rows_in, 3 * HW :].reshape(NX * rows_in, ffx), down_low], axis=0
    )
    early, late = pair_z(early), pair_z(late)
    early = order_y(at, gather_rel(early, "y"))
    late = gather_rel(late, "y")
    w_out = early[:, :, NX * lines :].reshape(HW, D)
    cols = early[:, :, : NX * lines].reshape(NY, NZ, NX, lines, 3 * HW)
    w_qkv = whole_rows(cols[:, :, :, :rows_in])
    info = cols[:, :, :, rows_in:, : 128 + gain_cols].astype(f32)
    gain = info[:, :, :, :3, 128:]
    gain = jnp.transpose(gain, (3, 2, 0, 1, 4)).reshape(3, D)
    frequency = jnp.exp(jnp.arange(HD // 2, dtype=f32) * (-math.log(10000.0) / (HD // 2)))
    frequency = jnp.broadcast_to(frequency[:, None], (HD // 2, 128))
    columns, lists, places, tokens_y, tokens_x, counts, cosine, sine = prep(
        at, info[..., :128].reshape(shards, lines - rows_in, 128), key_bases, frequency
    )
    counts = counts[:NDOM, 0]
    targets_row = lists[:, :PAD].astype(i32)

    found = lookup(bases_x, columns, 0, table)
    w_outs = lax.all_gather(tie(w_out, table), "x")
    wanted = lookup(tie(bases_x, found), columns, 2, table)
    parts = scatter_rel([found[k * NZ * PIECE : (k + 1) * NZ * PIECE] for k in range(NY)], "y")
    parts, wanted, late = lax.optimization_barrier((parts, wanted, late))
    late = order_y(at, late)
    split = NX * rows_in
    w_up = whole_rows(late[:, :, :split].reshape(NY, NZ, NX, rows_in, ffx))
    w_dn = late[:, :, split:].reshape(ffx, D)
    found = sum32(parts).astype(bf16)
    x0_own = sum32(scatter_rel([found[:PIECE], found[PIECE:]], "z"))
    x0_pieces = gather_rel(x0_own.astype(bf16), "x")

    x0, a, q, kv = qkv(x0_pieces, gain[0:1], w_qkv, cosine, sine)
    kvs = gather_rel(kv, "y")
    lead = delta_down.shape[1]
    delta_tail = jnp.concatenate(
        [delta_down[0], jnp.pad(delta_gains[0], ((0, 5), (0, D - gain_cols)))], axis=0
    )
    summed = lax.psum((delta_embed[0], delta_rows[0], delta_tail), ("zh", "c"))
    wanted = tie(wanted, (kvs, summed))
    wanted = lax.psum_scatter(wanted, "y", scatter_dimension=0, tiled=True)
    o, lse_q = attend(key_bases, q, kvs, places)
    os = gather_rel(o, "x")
    x1 = x0.astype(f32)
    for s, heads in enumerate(os):
        pieces = [heads[((j - s) % NX) * PIECE : ((j - s) % NX + 1) * PIECE] for j in range(NX)]
        heads = jnp.concatenate(pieces, axis=0) if s else heads
        x1 = x1 + mm(heads, lax.dynamic_index_in_dim(w_outs, (xi - s) % NX, 0, False))

    b = rms_norm(x1, gain[1]).astype(bf16)
    up = mm(b, w_up)
    hmid = jax.nn.gelu(up).astype(bf16)
    part = mm(hmid, w_dn).astype(bf16).reshape(NX, PIECE, D)
    parts = scatter_rel([part[k] for k in range(NX)], "x")
    target_rows = scatter_rel([wanted[:PIECE], wanted[PIECE:]], "z")
    parts, target_rows = lax.optimization_barrier((parts, target_rows))
    x2 = x1[:PIECE] + sum32(parts)
    hf = rms_norm(x2, gain[2]).astype(bf16)

    hf_pair = jnp.concatenate(gather_rel(hf, "z"), axis=0)
    states = gather_ring(hf_pair, "y")
    summed = tie(summed, hf_pair)
    summed = (summed[0], summed[1], summed[2][:lead], summed[2][lead : lead + 3, :gain_cols])
    group_count = lax.axis_size("zh") * lax.axis_size("c")
    weights_now = (embedding[0], w_rows[0], w_down[0], norm_gains[0])
    outers = (outer_embed, outer_rows, outer_down, outer_gains)
    means = [part_sum / group_count for part_sum in summed]
    momenta = [OUTER_MU * outer + mean for outer, mean in zip(outers, means)]
    starts = []
    for kind_index in range(4):
        shrink = 1.0 - (0.0 if kind_index == 3 else RATE * DECAY)
        starts.append(
            shrink * weights_now[kind_index]
            - OUTER_RATE * (means[kind_index] + OUTER_MU * momenta[kind_index])
        )

    states, means, momenta, starts = lax.optimization_barrier((states, means, momenta, starts))
    *rest_sum, stats = head(count, bases_x, states, table, columns)
    stats = lax.all_to_all(stats, ("y", "z"), 0, 0, tiled=True)
    terms = [rest_sum[0]]
    for index in range(1, NY * NZ):
        ky, kz = index // NZ, index % NZ
        perm = [
            (y * NZ + z, ((y - ky) % NY) * NZ + (z - kz) % NZ)
            for y in range(NY)
            for z in range(NZ)
        ]
        terms.append(lax.ppermute(rest_sum[index], ("y", "z"), perm))
    stats, scales, sums_own = merge(at, stats, lists)
    def head_grad(first, many, after, before=None):
        return table_grad(
            first, many, tie(bases_x, after), table, states, targets_row, stats, before
        )

    from_head = head_grad(0, 2, stats)
    terms, from_head = lax.optimization_barrier((terms, from_head))
    d_hf = -scales[:, NY * NZ : NY * NZ + 1] * sum32(target_rows)
    for index, term in enumerate(terms):
        d_hf = d_hf + scales[:, index : index + 1] * term.astype(f32)

    dx2, gain_two = rms_back(x2, gain[2], d_hf)
    dx2_low = dx2.astype(bf16)
    g2 = gather_rel(dx2_low, "x")
    from_head = head_grad(2, 1, dx2_low, from_head)
    g2, from_head = lax.optimization_barrier((g2, from_head))
    g2 = jnp.concatenate(g2, axis=0)
    unused, pull_gelu = jax.vjp(jax.nn.gelu, up)
    d_up = pull_gelu(mm_nt(g2, w_dn))[0].astype(bf16)
    part = mm_nt(d_up, w_up).astype(bf16)
    d_b = scatter_rel([part[k * PIECE : (k + 1) * PIECE] for k in range(NX)], "x")

    def to_yz(value):
        value = value.astype(bf16).reshape(NX, NY * NZ, rows_in, value.shape[1])
        return jnp.transpose(value, (1, 0, 2, 3)).reshape(NY * NZ, NX * rows_in, -1)

    def scatter_yz(value):
        value = lax.all_to_all(value, ("y", "z"), 0, 0, tiled=True)
        return sum32([value[k] for k in range(NY * NZ)])

    from_head = head_grad(3, 1, part, from_head)
    d_b, from_head = lax.optimization_barrier((d_b, from_head))
    d_b = sum32(d_b)

    d_norm, gain_one = rms_back(x1[:PIECE], gain[1], d_b)
    dx1 = dx2 + d_norm
    dx1_low = dx1.astype(bf16)
    g1 = gather_rel(dx1_low, "x")
    g2_low, d_up_low = tie((g2, d_up), dx1_low)
    ffn_grad = jnp.concatenate(
        [
            to_yz(mm_tn(b, d_up_low)),
            mm_tn(hmid, g2_low).astype(bf16).reshape(NY * NZ, -1, D),
        ],
        axis=1,
    )
    g1, ffn_grad = lax.optimization_barrier((g1, ffn_grad))
    from_head = lax.psum_scatter(
        tie(from_head, dx1_low), "x", scatter_dimension=0, tiled=True
    )
    ffn_grad = ffn_grad.reshape(NY, NZ, -1, D)
    ffn_own = lax.dynamic_index_in_dim(ffn_grad, zi, 1, False)
    ffn_other = shift(lax.dynamic_index_in_dim(ffn_grad, 1 - zi, 1, False), "z", 1)
    dq, *dkvs = attend_back(key_bases, q, kvs, places, lse_q, g1, w_out)
    g1_low = jnp.concatenate(tie(g1, dkvs[0]), axis=0)
    out_grad = mm_tn(o, g1_low).astype(bf16)
    dkvs = scatter_rel(dkvs, "y")
    dkvs, out_grad = lax.optimization_barrier((dkvs, out_grad))
    d_mixed, part, gain_zero = qkv_back(dq, dkvs, cosine, sine, w_qkv, x0)
    d_a = scatter_rel([part[k * PIECE : (k + 1) * PIECE] for k in range(NX)], "x")
    d_a, ffn_other = lax.optimization_barrier((d_a, ffn_other))
    qkv_grad = to_yz(mm_tn(a, tie(d_mixed, d_a)))
    gains_grad = jnp.stack(tie([gain_zero[0], gain_one, gain_two], d_a))
    gains_grad = gains_grad.reshape(3, NX, NY * NZ, gain_cols).transpose(2, 1, 0, 3)
    gains_grad = gains_grad.reshape(NY * NZ, -1)
    high = lax.reduce_precision(gains_grad, 8, 7)
    gains_grad = jnp.concatenate([high, gains_grad - high], axis=1)
    gains_grad = jnp.pad(gains_grad[:, None, :], ((0, 0), (0, 15), (0, 0)))
    out_grad = tie(out_grad, d_a).reshape(NY * NZ, rows_in, D)
    out_rest = jnp.pad(out_grad[:, :, 3 * HW :], ((0, 0), (0, 0), (0, 6 * HW - D)))
    qkv_grad = jnp.concatenate(
        [qkv_grad, out_grad[:, :, : 3 * HW], out_rest, gains_grad.astype(bf16)], axis=1
    )
    ffn_grad = (ffn_own.astype(f32) + ffn_other.astype(f32)).astype(bf16)
    d_norm, unused = rms_back(x0_own, gain[0], sum32(d_a))
    gz = (dx1 + d_norm).astype(bf16)

    gz_pair, by_x = lax.optimization_barrier(
        (gather_rel(gz[:, :LEFT], "z"), gather_rel(gz[:, LEFT:], "y"))
    )
    gz_pair, by_x = jnp.concatenate(gz_pair, axis=0), jnp.concatenate(by_x, axis=0)
    qkv_grad = lax.all_to_all(tie(qkv_grad, gz), ("y", "z"), 0, 0, tiled=True)
    by_x, by_y = gather_rel(by_x, "z"), gather_rel(gz_pair, "x")
    by_x, by_y = lax.optimization_barrier((by_x, by_y))
    by_x = lax.all_gather(jnp.concatenate(by_x, axis=0), "x", axis=0, tiled=True)
    ffn_grad = lax.psum_scatter(
        tie(ffn_grad, (from_head, by_y)).reshape(-1, D), "y", scatter_dimension=0, tiled=True
    )
    by_y = gather_ring(jnp.concatenate(by_y, axis=0), "y")
    base_own = (mine * count).reshape(1)

    ffn_own = ffn_grad.astype(f32)
    split = NX * rows_in
    down_own = ffn_own[split:]
    cols_grad, out_own = sum_yz(qkv_grad, ffn_own[:split])
    cols_grad = lax.all_to_all(cols_grad, "x", 0, 0, tiled=True)
    rows_own, gains_own, sums = rows_grad(cols_grad, out_own, down_own, sums_own)
    gains_own = gains_own.reshape(3, gain_cols)

    left = embed_part(
        count, base_own, tokens_y, [by_y[0], by_y[1], by_y[4]], (0, PAD, 3 * PAD)
    )
    right = embed_part(count, base_own, tokens_x, [by_x], (0,))
    halves, left, right, sums = lax.optimization_barrier((by_y[2:4], left, right, sums))
    table, totals = embed_end(
        count, base_own, tokens_y, halves, left, right, from_head, sums
    )

    gradients = (table[:count], rows_own, down_own, gains_own)
    totals = all_sum(totals)
    domain_sums = totals[4, :NDOM]
    size_now = jnp.sqrt(totals[0, 0])
    factor = jnp.minimum(1.0, CLIP / size_now)

    firsts = (first_embed[0], first_rows[0], first_down[0], first_gains[0])
    seconds = (second_embed[0], second_rows[0], second_down[0], second_gains[0])
    new_items, moment_items, square_items = ([], [], [])
    for kind_index in range(4):
        moved, moment_new, square_new = adam(
            starts[kind_index],
            gradients[kind_index] * factor,
            firsts[kind_index],
            seconds[kind_index],
            GAIN_RATE if kind_index == 3 else RATE,
        )
        new_items.append(moved[None])
        moment_items.append(moment_new[None])
        square_items.append(square_new[None])
    return (
        domain_sums[None],
        counts[None],
        size_now.reshape(1),
        *new_items,
        *moment_items,
        *square_items,
        *means,
        *momenta,
    )


def solution(mesh):
    groups = mesh.shape["group"]
    high = 2 if groups % 2 == 0 else 1
    fine = Mesh(
        mesh.devices.reshape(high, groups // high, NX, NY, NZ), ("zh", "c", "x", "y", "z")
    )
    group, blk = ("zh", "c"), ("x", "y", "z")
    tokens = P(group, None, blk)
    rows = P(group, blk, None)
    gains = P(group, None, blk)
    kind = (rows, rows, rows, gains)
    shared = (P(blk, None), P(blk, None), P(blk, None), P(None, blk))
    return jax.shard_map(
        per_device,
        mesh=fine,
        in_specs=(tokens,) * 4 + kind * 4 + shared,
        out_specs=(P(group, None), P(group, None), P(group)) + kind * 3 + shared * 2,
        check_vma=False,
    )
```
